32 devices in a mesh: sx: 8 (over z, core), sy: 4 (over y, x).
Axes of the slice: x: 2, y: 2, z: 4, core: 2. Of those that a mesh axis runs over, the one named last changes fastest.
Arguments:
- right_sides: float32 [256, 32, 128], P(('sx', 'sy')), may hold values from -16 to 16
- tiles: bfloat16 [256, 7, 128, 128], P(('sx', 'sy')), may hold values from -1 to 1
- tile_cols: int32 [256, 6], P(('sx', 'sy')), may hold values from 0 to 15
- send_rows: int32 [128, 2], P(('sx', 'sy')), may hold values from 0 to 7
- block_inverse: bfloat16 [256, 128, 128], P(('sx', 'sy')), may hold values from -1 to 1
- coarse_basis: bfloat16 [256, 32, 128], P(('sx', 'sy')), may hold values from -0.1875 to 0.1875
- coarse_inverse: float32 [1024, 1024], P(('sx', 'sy')), may hold values from -4 to 4, as said below
Outputs:
- solution: float32 [256, 32, 128], P(('sx', 'sy'))
- residual: float32 [256, 32, 128], P(('sx', 'sy'))
The draws below stay inside these ranges and needn't reach their ends.
Inputs may be any that keep to these rules, and one draw needn't show every extreme that they name: coarse_inverse is symmetric: entry (i, j) equals entry (j, i).
All inputs are finite; a program needn't handle non-finite values.
Results may differ from the reference program's by a relative error of at most 0.012.
Values may be sent and summed in bfloat16 or wider, within the bound.
No kernel may reach another device: no remote copies, remote signals or barrier semaphores. Data moves between devices by JAX's collectives and lax.ppermute only.
A program may use at most 64 MiB of HBM per device.

```python
import math
import jax
import jax.numpy as jnp
from jax import lax

TILE = 128
NRHS = 32
KC = 32
NB = 8
HALO = 2
NBT = 256
KT = 1024
N_SX = 8
N_SY = 4
DEVICES = 32


def signed_hadamard(key):
    row_key, col_key = jax.random.split(jax.random.fold_in(key, 41))
    row_signs = (2 * jax.random.randint(row_key, (NBT, TILE), 0, 2) - 1).astype(jnp.float32)
    col_signs = (2 * jax.random.randint(col_key, (NBT, TILE), 0, 2) - 1).astype(jnp.float32)
    index = jnp.arange(TILE, dtype=jnp.int32)
    common = jnp.bitwise_and(index[:, None], index[None, :])
    parity = jnp.zeros((TILE, TILE), jnp.int32)
    for level in range(TILE.bit_length() - 1):
        parity = parity + jnp.bitwise_and(jnp.right_shift(common, level), 1)
    hadamard = (1 - 2 * (parity % 2)).astype(jnp.float32)
    return row_signs[:, :, None] * hadamard[None] * col_signs[:, None, :] * (1.0 / math.sqrt(TILE))


def draw_tiles(key, part):
    basis = signed_hadamard(key)
    first, second = jax.random.split(jax.random.fold_in(key, 53))
    diag_scale = 0.25 / math.sqrt(TILE)
    off_scale = 0.35 / math.sqrt(6 * TILE)
    diag_noise = jnp.clip(jax.random.normal(first, (NBT, TILE, TILE), jnp.float32), -5.0, 5.0) * diag_scale
    off_tiles = jnp.clip(jax.random.normal(second, (NBT, 6, TILE, TILE), jnp.float32), -5.0, 5.0) * off_scale
    diagonal = jnp.swapaxes(basis, 1, 2) + diag_noise
    return jnp.concatenate([diagonal[:, None], off_tiles], axis=1).astype(jnp.bfloat16)


def draw_block_inverse(key, part):
    basis = signed_hadamard(key)
    first = jax.random.fold_in(key, 67)
    noise_scale = 0.15 / math.sqrt(TILE)
    noise = jnp.clip(jax.random.normal(first, (NBT, TILE, TILE), jnp.float32), -5.0, 5.0) * noise_scale
    return (basis + noise).astype(jnp.bfloat16)


def draw_coarse_inverse(key, part):
    first = jax.random.fold_in(jax.random.fold_in(key, 11), 0)
    base = jnp.clip(jax.random.normal(first, (KT, KT), jnp.float32), -5.0, 5.0)
    symmetric = (base + base.T) * (1.4142 / math.sqrt(KT))
    diagonal = jnp.arange(KT)
    return symmetric.at[diagonal, diagonal].add(1.0)


def draw_right_sides(key, part):
    first = jax.random.fold_in(jax.random.fold_in(key, 23), 0)
    ramp = 3.0 ** (jnp.arange(NBT, dtype=jnp.float32) / max(NBT - 1, 1))
    ramp = ramp[:, None, None]
    base = jnp.clip(jax.random.normal(first, (NBT, NRHS, TILE), jnp.float32), -5.0, 5.0)
    return base * ramp


def with_ends(drawn, stream_key, low, largest):
    place = [jax.random.randint(jax.random.fold_in(stream_key, axis), (), 0, length) for axis, length in enumerate(drawn.shape)]
    longest = drawn.shape.index(max(drawn.shape))
    neighbour = place[:longest] + [(place[longest] + 1) % drawn.shape[longest]] + place[longest + 1:]
    return drawn.at[tuple(place)].set(low).at[tuple(neighbour)].set(largest)


def steps_of(key, shape, cuts, low, largest):
    loudness, own = 1.0, jax.random.fold_in(key, 6)
    for position, shards_of in cuts:
        draws = jnp.exp(jax.random.uniform(jax.random.fold_in(own, position), (shards_of,), jnp.float32, low / len(cuts), largest / len(cuts)))
        loudness = loudness * jnp.repeat(draws, shape[position] // shards_of).reshape([-1 if axis == position else 1 for axis in range(len(shape))])
    return loudness


def bell_draw(rng, extent, width, reach, shards=(), held_as=jnp.bfloat16):
    level = steps_of(rng, extent, shards, -0.22, 0.18) if shards else 1.0
    values = jax.random.normal(rng, extent, jnp.float32) * width * level
    return jnp.minimum(jnp.maximum(values, -reach), reach).astype(held_as)


def setup_inputs(seed: int = 0) -> dict:
    key_of = jax.random.split(jax.random.key(seed), 8)
    return {
        "right_sides": draw_right_sides(jax.random.fold_in(key_of[7], 71), 0),
        "tiles": draw_tiles(jax.random.fold_in(key_of[7], 71), 0),
        "tile_cols": with_ends(jax.random.randint(key_of[2], (NBT, 6), 0, NB + 4 * HALO), jax.random.fold_in(key_of[2], 1), 0, (NB + 4 * HALO) - 1).astype(jnp.int32),
        "send_rows": with_ends(jax.random.randint(key_of[3], (4 * DEVICES, HALO), 0, NB), jax.random.fold_in(key_of[3], 1), 0, NB - 1).astype(jnp.int32),
        "block_inverse": draw_block_inverse(jax.random.fold_in(key_of[7], 71), 0),
        "coarse_basis": bell_draw(key_of[5], (NBT, KC, TILE), (NB * TILE) ** -0.5, 0.1875, ((0, 32),)),
        "coarse_inverse": draw_coarse_inverse(jax.random.fold_in(key_of[7], 71), 0),
    }


def pick_rows(block_grid, chosen):
    return block_grid[chosen]


def apply_operator(packed, tiles, tile_cols, send_rows):
    grid = packed.reshape(N_SX, N_SY, NB, NRHS, TILE)
    rows = send_rows.reshape(N_SX, N_SY, 4, HALO)
    outgoing = jax.vmap(jax.vmap(pick_rows))(grid, rows)
    zero_row = jnp.zeros_like(outgoing[:1, :, 0])
    from_below = jnp.concatenate([zero_row, outgoing[:-1, :, 0]], axis=0)
    from_above = jnp.concatenate([outgoing[1:, :, 1], zero_row], axis=0)
    zero_col = jnp.zeros_like(outgoing[:, :1, 2])
    from_left = jnp.concatenate([zero_col, outgoing[:, :-1, 2]], axis=1)
    from_right = jnp.concatenate([outgoing[:, 1:, 3], zero_col], axis=1)
    extended = jnp.concatenate([grid, from_below, from_above, from_left, from_right], axis=2)
    extended = extended.reshape(N_SX * N_SY, NB + 4 * HALO, NRHS, TILE)
    tiles_dev = tiles.reshape(N_SX * N_SY, NB, 7, TILE, TILE)
    cols_dev = tile_cols.reshape(N_SX * N_SY, NB, 6)

    def device_product(operands):
        ext_blocks, own_tiles, own_cols = operands
        picked = ext_blocks[own_cols]
        stacked = jnp.concatenate([ext_blocks[:NB, None], picked], axis=1)
        return jnp.einsum("btik,btrk->bri", own_tiles.astype(jnp.float32), stacked.astype(jnp.float32), precision=lax.Precision.HIGHEST)

    result = lax.map(device_product, (extended, tiles_dev, cols_dev))
    return result.reshape(NBT, NRHS, TILE)


def coarse_solve(vector, coarse_basis, coarse_inverse):
    basis = coarse_basis.reshape(N_SX * N_SY, NB, KC, TILE).astype(jnp.float32)
    restricted = jnp.einsum("dbki,dbri->dkr", basis, vector.reshape(N_SX * N_SY, NB, NRHS, TILE), precision=lax.Precision.HIGHEST)
    coarse = jnp.dot(coarse_inverse, restricted.reshape(KT, NRHS), precision=lax.Precision.HIGHEST)
    return coarse.reshape(N_SX * N_SY, KC, NRHS)


def precondition(vector, coarse, block_inverse, coarse_basis):
    rounded = vector.astype(jnp.bfloat16).astype(jnp.float32)
    local = jnp.einsum("bik,brk->bri", block_inverse.astype(jnp.float32), rounded, precision=lax.Precision.HIGHEST)
    basis = coarse_basis.reshape(N_SX * N_SY, NB, KC, TILE).astype(jnp.float32)
    coarse_low = coarse.astype(jnp.bfloat16).astype(jnp.float32)
    spread = jnp.einsum("dbki,dkr->dbri", basis, coarse_low, precision=lax.Precision.HIGHEST)
    return local + spread.reshape(NBT, NRHS, TILE)


def reference(right_sides, tiles, tile_cols, send_rows, block_inverse, coarse_basis, coarse_inverse):
    residual = right_sides
    solution = jnp.zeros_like(right_sides)
    for step in range(2):
        coarse = coarse_solve(residual, coarse_basis, coarse_inverse)
        update = precondition(residual, coarse, block_inverse, coarse_basis)
        packed = update.astype(jnp.bfloat16)
        image = apply_operator(packed, tiles, tile_cols, send_rows)
        upper = jnp.sum(residual * image, axis=(0, 2))
        lower = jnp.sum(image * image, axis=(0, 2))
        weight = upper / (lower + 1e-6)
        solution = solution + weight[None, :, None] * update
        residual = residual - weight[None, :, None] * image
    return solution, residual
```

```python
import jax
import jax.numpy as jnp
from jax import lax
from jax.sharding import PartitionSpec as P

AXES = ("sx", "sy")
BF = jnp.bfloat16
F32 = jnp.float32


def swap(value, axis, odd):
    count = lax.axis_size(axis)
    pairs = []
    for place in range(count):
        step = 1 if (place % 2 == 0) != odd else -1
        pairs.append((place, (place + step) % count))
    return lax.ppermute(value, axis, pairs)


def swap_plan():
    plan = []
    for number, axis in enumerate(AXES):
        place, count = lax.axis_index(axis), lax.axis_size(axis)
        for odd in (False, True):
            up = (place % 2 == 0) != odd
            valid = jnp.where(up, place < count - 1, place > 0)
            plan.append((axis, odd, 2 * number + jnp.where(up, 0, 1), 2 * number + jnp.where(up, 1, 0), valid))
    return plan


def split(value):
    high = value.astype(BF)
    return high, (value - high.astype(F32)).astype(BF)


def local_part(vector, block_inverse):
    return sum(
        jnp.einsum("bik,brk->bri", block_inverse, part, preferred_element_type=F32) for part in split(vector)
    )


def restrict(vector, coarse_basis):
    high, low = split(vector)
    return sum(jnp.einsum("bki,bri->kr", coarse_basis, part, preferred_element_type=F32) for part in (high, low))


def spread(coarse, basis):
    return jnp.einsum("ski,skr->sri", basis, coarse.astype(BF), preferred_element_type=F32)


def gather(slot):
    count = lax.axis_size("sx") * lax.axis_size("sy")
    return lax.all_to_all(jnp.broadcast_to(slot[None], (count,) + slot.shape), AXES, 0, 0, tiled=True)


def image_of(packed, tiles, tile_cols):
    stacked = jnp.concatenate([packed[:8, None], packed[tile_cols]], axis=1)
    return jnp.einsum("btik,btrk->bri", tiles, stacked, preferred_element_type=F32)


def body(right_sides, tiles, tile_cols, send_rows, block_inverse, coarse_basis, coarse_inverse):
    blocks, rhs, order = right_sides.shape
    vectors = coarse_basis.shape[1]
    plan = swap_plan()

    def exchange(buffers):
        arrived = [swap(lax.dynamic_index_in_dim(buffers, send, 0, False), axis, odd) for axis, odd, send, _, _ in plan]
        arrived = [jnp.where(valid, value, 0) for value, (_, _, _, _, valid) in zip(arrived, plan)]
        up = [plan[0][3] == 1, plan[2][3] == 3]
        return [
            jnp.where(up[0], arrived[1], arrived[0]),
            jnp.where(up[0], arrived[0], arrived[1]),
            jnp.where(up[1], arrived[3], arrived[2]),
            jnp.where(up[1], arrived[2], arrived[3]),
        ]

    halo = send_rows.shape[1]
    inverse = coarse_inverse.astype(BF)
    local0 = local_part(right_sides, block_inverse)
    first = jnp.concatenate(
        [
            jnp.broadcast_to(inverse.reshape(1, -1, order), (4, inverse.size // order, order)),
            coarse_basis[send_rows].reshape(4, halo * vectors, order),
            local0.astype(BF)[send_rows].reshape(4, halo * rhs, order),
        ],
        axis=1,
    )
    slot = restrict(right_sides, coarse_basis).astype(BF).reshape(-1, order)
    restricted = gather(slot).reshape(-1, rhs)
    received = exchange(first)
    rows = inverse.size // order
    inverses = jnp.concatenate([inverse] + [value[:rows].reshape(inverse.shape) for value in received], axis=0)
    basis = jnp.concatenate(
        [coarse_basis] + [value[rows : rows + halo * vectors].reshape(halo, vectors, order) for value in received]
    )
    local0 = jnp.concatenate(
        [local0] + [value[rows + halo * vectors :].reshape(halo, rhs, order).astype(F32) for value in received]
    )

    def coarse_part(restricted):
        coarse = jnp.dot(inverses, restricted, preferred_element_type=F32).reshape(5, vectors, rhs)
        chosen = jnp.concatenate(
            [jnp.broadcast_to(coarse[0], (blocks, vectors, rhs)), jnp.repeat(coarse[1:], halo, axis=0)], axis=0
        )
        return spread(chosen, basis)

    update = local0 + coarse_part(restricted)
    image = image_of(update.astype(BF), tiles, tile_cols)

    sums = jnp.stack([jnp.sum(right_sides * image, axis=(0, 2)), jnp.sum(image * image, axis=(0, 2))])
    high, low = split(sums)
    slot = jnp.concatenate(
        [
            restrict(image, coarse_basis).astype(BF).reshape(-1, order),
            jnp.concatenate([high.reshape(1, -1), low.reshape(1, -1)], axis=1),
            jnp.zeros((7, order), BF),
        ]
    )
    arrived = gather(slot)
    local1 = local_part(image, block_inverse)
    received = exchange(local1.astype(BF)[send_rows].reshape(4, halo * rhs, order))
    restricted = arrived[:, :-8].reshape(-1, rhs)
    sums = jnp.sum(arrived[:, -8].astype(F32), axis=0).reshape(2, 2, rhs).sum(axis=0)
    weight = (sums[0] / (sums[1] + 1e-6))[None, :, None]
    local1 = jnp.concatenate([local1] + [value.reshape(halo, rhs, order).astype(F32) for value in received])
    second = update - weight * (local1 + coarse_part(restricted))
    residual = right_sides - weight * image
    image2 = image_of(second.astype(BF), tiles, tile_cols)
    sums = jnp.stack([jnp.sum(residual * image2, axis=(0, 2)), jnp.sum(image2 * image2, axis=(0, 2))])
    slot = jnp.concatenate([sums.reshape(1, -1), jnp.zeros((1, order - 2 * rhs), F32)], axis=1)
    sums = jnp.sum(gather(slot), axis=(0, 1))[: 2 * rhs].reshape(2, rhs)
    weight2 = (sums[0] / (sums[1] + 1e-6))[None, :, None]
    return weight * update[:blocks] + weight2 * second[:blocks], residual - weight2 * image2


def solution(mesh):
    block3 = P(AXES, None, None)
    placed = (block3, P(AXES, None, None, None), P(AXES, None), P(AXES, None), block3, block3, P(AXES, None))
    return jax.shard_map(body, mesh=mesh, in_specs=placed, out_specs=(block3, block3), check_vma=False)
```

```python
import functools

import jax
import jax.numpy as jnp
from jax import lax
from jax.experimental import pallas as pl
from jax.experimental.pallas import tpu as pltpu
from jax.sharding import PartitionSpec as P

AXES = ("sx", "sy")
BF = jnp.bfloat16
F32 = jnp.float32
NT = (((1,), (1,)), ((), ()))
LANES = 128
SLOT = 8
SWAPS = tuple((axis, odd) for axis in range(2) for odd in (False, True))


def swap(value, axis, odd):
    count = lax.axis_size(axis)
    pairs = []
    for place in range(count):
        step = 1 if (place % 2 == 0) != odd else -1
        pairs.append((place, (place + step) % count))
    return lax.ppermute(value, axis, pairs)


def swap_ends(number, odd):
    axis = AXES[number]
    place, count = lax.axis_index(axis), lax.axis_size(axis)
    up = (lax.rem(place, 2) == 0) != odd
    send = 2 * number + jnp.where(up, 0, 1)
    slot = 2 * number + jnp.where(up, 1, 0)
    valid = jnp.where(up, place < count - 1, place > 0)
    return send, slot, valid


def split(value):
    high = value.astype(BF)
    return high, (value - high.astype(F32)).astype(BF)


def restrict_slot(vectors, basis_ref):
    left, right = [], []
    for b, vector in enumerate(vectors):
        for part in split(vector):
            left.append(basis_ref[b])
            right.append(jnp.concatenate([part] * 4, axis=0))
    full = lax.dot_general(
        jnp.concatenate(left, axis=1), jnp.concatenate(right, axis=1), NT, preferred_element_type=F32
    )
    group = lax.broadcasted_iota(jnp.int32, (SLOT, LANES), 1) // 32
    slot = full[:SLOT]
    for j in range(1, 4):
        slot = jnp.where(group == j, full[SLOT * j : SLOT * (j + 1)], slot)
    return slot


def coarse_parts(arrived, inverses):
    count = arrived.shape[0]
    lane = lax.broadcasted_iota(jnp.int32, (1, 4, SLOT, LANES), 3) // 32
    part = lax.broadcasted_iota(jnp.int32, (1, 4, SLOT, LANES), 1)
    spread_out = jnp.where(lane == part, arrived[:, None].astype(F32), 0.0)
    column = spread_out.reshape(count * 4 * SLOT, LANES).astype(BF)
    product = jnp.dot(jnp.concatenate(inverses, axis=0), column, preferred_element_type=F32)
    parts = []
    for s in range(len(inverses)):
        turned = product[32 * s : 32 * (s + 1)].T
        parts.append((turned[:32] + turned[32:64] + turned[64:96] + turned[96:]).astype(BF))
    return parts


def local_product(vector, inverse):
    rows = vector.shape[0]
    both = lax.dot_general(jnp.concatenate(split(vector), axis=0), inverse, NT, preferred_element_type=F32)
    return both[:rows] + both[rows:]


def image_block(b, extended, tiles, cols_ref):
    vectors = [extended[b]] + [extended[cols_ref[b, t]] for t in range(tiles.shape[1] - 1)]
    blocks = [tiles[b, t] for t in range(tiles.shape[1])]
    return lax.dot_general(
        jnp.concatenate(vectors, axis=1), jnp.concatenate(blocks, axis=1), NT, preferred_element_type=F32
    )


def sums_row(upper, lower):
    return jnp.sum(jnp.concatenate([upper, lower, upper, lower], axis=0).T, axis=0, keepdims=True)


def start_tiles(tiles_hbm, tiles, sems):
    copies = [pltpu.make_async_copy(tiles_hbm.at[b], tiles.at[b], sems.at[b]) for b in range(tiles.shape[0])]
    for copy in copies:
        copy.start()
    return copies


def restrict_kernel(right_ref, basis_ref, slot_ref):
    vectors = [right_ref[b] for b in range(right_ref.shape[0])]
    slot_ref[...] = jnp.broadcast_to(restrict_slot(vectors, basis_ref).astype(BF)[None], slot_ref.shape)


def first_halo_kernel(send_ref, right_ref, block_inverse_ref, basis_ref, inverse_ref, local_ref, *out_refs):
    blocks, rhs, order = right_ref.shape
    halo = send_ref.shape[1]
    total = inverse_ref.shape[1]
    for b in range(blocks):
        local_ref[b] = local_product(right_ref[b], block_inverse_ref[b])
    inverse = inverse_ref[...].astype(BF)
    for (number, odd), out_ref in zip(SWAPS, out_refs):
        send, _, _ = swap_ends(number, odd)
        out_ref[:, :total] = inverse
        for m in range(halo):
            row = send_ref[send, m]
            out_ref[:, total + m * order : total + (m + 1) * order] = basis_ref[row]
            start = total + (halo + m) * order
            out_ref[:, start : start + order] = local_ref[row].astype(BF)


def first_image_kernel(
    cols_ref, arrived_ref, inverse_ref, halo0, halo1, halo2, halo3, basis_ref, local_ref, right_ref, tiles_hbm,
    slot_ref, update_ref, image_ref,
    tiles, extended, sems,
):
    copies = start_tiles(tiles_hbm, tiles, sems)
    blocks, rhs, order = right_ref.shape
    total = inverse_ref.shape[1]
    halos = (halo0, halo1, halo2, halo3)
    halo = (halo0.shape[1] - total) // (2 * order)
    inverses = [inverse_ref[...].astype(BF)] + [ref[:, :total] for ref in halos]
    coarse = coarse_parts(arrived_ref[...], inverses)
    for b in range(blocks):
        update = local_ref[b] + jnp.dot(coarse[0], basis_ref[b], preferred_element_type=F32)
        update_ref[b] = update
        extended[b] = update.astype(BF)
    for q, (number, odd) in enumerate(SWAPS):
        _, slot, valid = swap_ends(number, odd)
        for m in range(halo):
            basis = halos[q][:, total + m * order : total + (m + 1) * order]
            start = total + (halo + m) * order
            local = halos[q][:, start : start + order].astype(F32)
            update = local + jnp.dot(coarse[1 + q], basis, preferred_element_type=F32)
            update_ref[blocks + halo * q + m] = update
            extended[blocks + halo * slot + m] = jnp.where(valid, update, 0.0).astype(BF)
    upper = lower = jnp.zeros((rhs, order), F32)
    images = []
    for b in range(blocks):
        copies[b].wait()
        image = image_block(b, extended, tiles, cols_ref)
        image_ref[b] = image
        images.append(image)
        upper += right_ref[b] * image
        lower += image * image
    row = sums_row(upper, lower)
    high, low = split(row)
    lane = lax.broadcasted_iota(jnp.int32, (1, LANES), 1)
    row = jnp.where(lane < 64, high.astype(F32), low.astype(F32))
    whole = jnp.concatenate([restrict_slot(images, basis_ref), jnp.broadcast_to(row, (SLOT, LANES))], axis=0)
    slot_ref[...] = jnp.broadcast_to(whole.astype(BF)[None], slot_ref.shape)


def second_halo_kernel(send_ref, image_ref, block_inverse_ref, local_ref, *out_refs):
    blocks, rhs, order = image_ref.shape
    for b in range(blocks):
        local_ref[b] = local_product(image_ref[b], block_inverse_ref[b])
    for (number, odd), out_ref in zip(SWAPS, out_refs):
        send, _, _ = swap_ends(number, odd)
        for m in range(send_ref.shape[1]):
            out_ref[:, m * order : (m + 1) * order] = local_ref[send_ref[send, m]].astype(BF)


def second_image_kernel(
    cols_ref, arrived_ref, inverse_ref, halo0, halo1, halo2, halo3, next0, next1, next2, next3,
    basis_ref, local_ref, update_ref, image_ref, right_ref, tiles_hbm,
    slot_ref, scaled_ref, second_ref, residual_ref, image2_ref,
    tiles, extended, sems,
):
    copies = start_tiles(tiles_hbm, tiles, sems)
    blocks, rhs, order = right_ref.shape
    total = inverse_ref.shape[1]
    halos, nexts = (halo0, halo1, halo2, halo3), (next0, next1, next2, next3)
    halo = next0.shape[1] // order
    inverses = [inverse_ref[...].astype(BF)] + [ref[:, :total] for ref in halos]
    arrived = arrived_ref[...].astype(F32)
    coarse = coarse_parts(arrived[:, :SLOT], inverses)
    sums = jnp.sum(arrived[:, SLOT:], axis=0)
    turned = jnp.concatenate([sums] * (LANES // SLOT), axis=0).T
    weight = (turned[:32] + turned[64:96]) / (turned[32:64] + turned[96:] + 1e-6)
    for b in range(blocks):
        change = local_ref[b] + jnp.dot(coarse[0], basis_ref[b], preferred_element_type=F32)
        update = update_ref[b]
        second = update - weight * change
        scaled_ref[b] = weight * update
        second_ref[b] = second
        extended[b] = second.astype(BF)
    for q, (number, odd) in enumerate(SWAPS):
        _, slot, valid = swap_ends(number, odd)
        for m in range(halo):
            basis = halos[q][:, total + m * order : total + (m + 1) * order]
            local = nexts[q][:, m * order : (m + 1) * order].astype(F32)
            change = local + jnp.dot(coarse[1 + q], basis, preferred_element_type=F32)
            second = update_ref[blocks + halo * q + m] - weight * change
            extended[blocks + halo * slot + m] = jnp.where(valid, second, 0.0).astype(BF)
    upper = lower = jnp.zeros((rhs, order), F32)
    for b in range(blocks):
        residual = right_ref[b] - weight * image_ref[b]
        residual_ref[b] = residual
        copies[b].wait()
        image = image_block(b, extended, tiles, cols_ref)
        image2_ref[b] = image
        upper += residual * image
        lower += image * image
    slot_ref[...] = jnp.broadcast_to(sums_row(upper, lower)[None], slot_ref.shape)


def last_kernel(arrived_ref, scaled_ref, second_ref, residual_ref, image_ref, solution_ref, out_ref):
    sums = jnp.sum(arrived_ref[...], axis=0)
    turned = jnp.broadcast_to(sums, (LANES, LANES)).T
    weight = turned[:32] / (turned[32:64] + 1e-6)
    for b in range(scaled_ref.shape[0]):
        solution_ref[b] = scaled_ref[b] + weight * second_ref[b]
        out_ref[b] = residual_ref[b] - weight * image_ref[b]


def call(kernel, inputs, places, outputs, scratch=()):
    vmem, smem, anywhere = pltpu.VMEM, pltpu.SMEM, pl.ANY
    kinds = {"v": vmem, "s": smem, "a": anywhere}
    return pl.pallas_call(
        kernel,
        out_shape=[jax.ShapeDtypeStruct(shape, dtype) for shape, dtype in outputs],
        in_specs=[pl.BlockSpec(memory_space=kinds[place]) for place in places],
        out_specs=[pl.BlockSpec(memory_space=vmem)] * len(outputs),
        scratch_shapes=scratch,
        compiler_params=pltpu.CompilerParams(vmem_limit_bytes=48 * 1024 * 1024),
        name=kernel.__name__,
    )(*inputs)


def exchange(slots):
    return lax.all_to_all(slots, AXES, 0, 0, tiled=True)


def body(right_sides, tiles, tile_cols, send_rows, block_inverse, coarse_basis, coarse_inverse):
    blocks, rhs, order = right_sides.shape
    rows, total = coarse_inverse.shape
    halo = send_rows.shape[1]
    count = lax.axis_size("sx") * lax.axis_size("sy")
    field = ((blocks, rhs, order), F32)
    scratch = (
        pltpu.VMEM(tiles.shape, BF),
        pltpu.VMEM((blocks + 4 * halo, rhs, order), BF),
        pltpu.SemaphoreType.DMA((blocks,)),
    )

    (slots,) = call(restrict_kernel, (right_sides, coarse_basis), "vv", [((count, SLOT, LANES), BF)])
    arrived = exchange(slots)
    local, *halos = call(
        first_halo_kernel,
        (send_rows, right_sides, block_inverse, coarse_basis, coarse_inverse),
        "svvvv",
        [field] + [((rhs, total + 2 * halo * order), BF)] * 4,
    )
    halos = [swap(value, AXES[number], odd) for value, (number, odd) in zip(halos, SWAPS)]
    slots, update, image = call(
        first_image_kernel,
        (tile_cols, arrived, coarse_inverse, *halos, coarse_basis, local, right_sides, tiles),
        "svvvvvvvvva",
        [((count, 2 * SLOT, LANES), BF), ((blocks + 4 * halo, rhs, order), F32), field],
        scratch,
    )
    arrived = exchange(slots)
    local, *nexts = call(
        second_halo_kernel,
        (send_rows, image, block_inverse),
        "svv",
        [field] + [((rhs, halo * order), BF)] * 4,
    )
    nexts = [swap(value, AXES[number], odd) for value, (number, odd) in zip(nexts, SWAPS)]
    slots, scaled, second, residual, image = call(
        second_image_kernel,
        (tile_cols, arrived, coarse_inverse, *halos, *nexts, coarse_basis, local, update, image, right_sides, tiles),
        "svvvvvvvvvvvvvvva",
        [((count, 1, LANES), F32)] + [field] * 4,
        scratch,
    )
    return tuple(call(last_kernel, (exchange(slots), scaled, second, residual, image), "vvvvv", [field] * 2))


def solution(mesh):
    block3 = P(AXES, None, None)
    placed = (block3, P(AXES, None, None, None), P(AXES, None), P(AXES, None), block3, block3, P(AXES, None))
    return jax.shard_map(body, mesh=mesh, in_specs=placed, out_specs=(block3, block3), check_vma=False)
```

```python
import functools

import jax
import jax.numpy as jnp
from jax import lax
from jax.experimental import pallas as pl
from jax.experimental.pallas import tpu as pltpu
from jax.sharding import PartitionSpec as P

AXES = ("sx", "sy")
BF = jnp.bfloat16
F32 = jnp.float32
NT = (((1,), (1,)), ((), ()))
LANES = 128
SLOT = 8
SWAPS = ((1, True), (0, True), (1, False), (0, False))


def swap(value, axis, odd):
    count = lax.axis_size(axis)
    pairs = []
    for place in range(count):
        step = 1 if (place % 2 == 0) != odd else -1
        pairs.append((place, (place + step) % count))
    return lax.ppermute(value, axis, pairs)


def swap_ends(number, odd):
    axis = AXES[number]
    place, count = lax.axis_index(axis), lax.axis_size(axis)
    up = (lax.rem(place, 2) == 0) != odd
    send = 2 * number + jnp.where(up, 0, 1)
    slot = 2 * number + jnp.where(up, 1, 0)
    valid = jnp.where(up, place < count - 1, place > 0)
    return send, slot, valid


def split(value):
    high = value.astype(BF)
    return high, (value - high.astype(F32)).astype(BF)


def restrict_slot(vectors, basis_ref):
    left, right = [], []
    for b, vector in enumerate(vectors):
        for part in split(vector):
            left.append(basis_ref[b])
            right.append(jnp.concatenate([part] * 4, axis=0))
    full = lax.dot_general(
        jnp.concatenate(left, axis=1), jnp.concatenate(right, axis=1), NT, preferred_element_type=F32
    )
    group = lax.broadcasted_iota(jnp.int32, (SLOT, LANES), 1) // 32
    slot = full[:SLOT]
    for j in range(1, 4):
        slot = jnp.where(group == j, full[SLOT * j : SLOT * (j + 1)], slot)
    return slot


def coarse_parts(arrived, inverses):
    count = arrived.shape[0]
    lane = lax.broadcasted_iota(jnp.int32, (1, 4, SLOT, LANES), 3) // 32
    part = lax.broadcasted_iota(jnp.int32, (1, 4, SLOT, LANES), 1)
    spread_out = jnp.where(lane == part, arrived[:, None].astype(F32), 0.0)
    column = spread_out.reshape(count * 4 * SLOT, LANES).astype(BF)
    product = jnp.dot(jnp.concatenate(inverses, axis=0), column, preferred_element_type=F32)
    parts = []
    for s in range(len(inverses)):
        turned = product[32 * s : 32 * (s + 1)].T
        parts.append((turned[:32] + turned[32:64] + turned[64:96] + turned[96:]).astype(BF))
    return parts


def local_product(vector, inverse):
    rows = vector.shape[0]
    both = lax.dot_general(jnp.concatenate(split(vector), axis=0), inverse, NT, preferred_element_type=F32)
    return both[:rows] + both[rows:]


def image_block(b, extended, tiles, cols_ref):
    vectors = [extended[b]] + [extended[cols_ref[b, t]] for t in range(tiles.shape[1] - 1)]
    blocks = [tiles[b, t] for t in range(tiles.shape[1])]
    return lax.dot_general(
        jnp.concatenate(vectors, axis=1), jnp.concatenate(blocks, axis=1), NT, preferred_element_type=F32
    )


def sums_row(upper, lower):
    return jnp.sum(jnp.concatenate([upper, lower, upper, lower], axis=0).T, axis=0, keepdims=True)


def fetch(pairs, sems):
    copies = [pltpu.make_async_copy(source, target, sems.at[k]) for k, (source, target) in enumerate(pairs)]
    for copy in copies:
        copy.start()
    return copies


def start_kernel(
    send_hbm, right_hbm, block_inverse_hbm, basis_hbm, inverse_hbm,
    slot_hbm, right_ref, block_inverse_ref, basis_ref, inverse_ref, local_ref, out0, out1, out2, out3,
    slot_ref, out_ref, send_ref, wide, sems, out_sems,
):
    copies = fetch(
        [
            (right_hbm, right_ref),
            (basis_hbm, basis_ref),
            (block_inverse_hbm, block_inverse_ref),
            (inverse_hbm, wide),
            (send_hbm, send_ref),
        ],
        sems,
    )
    blocks, rhs, order = right_ref.shape
    halo = send_ref.shape[0]
    total = wide.shape[1]
    for copy in copies[:2]:
        copy.wait()
    vectors = [right_ref[b] for b in range(blocks)]
    slot_ref[...] = jnp.broadcast_to(restrict_slot(vectors, basis_ref).astype(BF)[None], slot_ref.shape)
    leaving = fetch([(slot_ref, slot_hbm)], out_sems)
    copies[2].wait()
    for b in range(blocks):
        local_ref[b] = local_product(right_ref[b], block_inverse_ref[b])
    copies[3].wait()
    inverse = wide[...].astype(BF)
    inverse_ref[...] = inverse
    copies[4].wait()
    for q, ((number, odd), out_hbm) in enumerate(zip(SWAPS, (out0, out1, out2, out3))):
        send, _, _ = swap_ends(number, odd)
        out_ref[q, :, :total] = inverse
        for m in range(halo):
            row = send_ref[m, send]
            out_ref[q, :, total + m * order : total + (m + 1) * order] = basis_ref[row]
            start = total + (halo + m) * order
            out_ref[q, :, start : start + order] = local_ref[row].astype(BF)
        leaving += fetch([(out_ref.at[q], out_hbm)], out_sems.at[pl.ds(1 + q, 1)])
    for copy in leaving:
        copy.wait()


def load_kernel(after_ref, tiles_hbm, tiles_ref, sems):
    for copy in fetch([(tiles_hbm.at[b], tiles_ref.at[b]) for b in range(tiles_ref.shape[0])], sems):
        copy.wait()


def first_kernel(
    cols_hbm, send_hbm, arrived_ref, inverse_ref, halo0, halo1, halo2, halo3,
    block_inverse_ref, basis_ref, local_ref, right_ref, tiles_ref,
    slot_hbm, update_ref, image_ref, next_local_ref, out0, out1, out2, out3,
    slot_ref, out_ref, cols_ref, send_ref, extended, sems, out_sems,
):
    copies = fetch([(cols_hbm, cols_ref), (send_hbm, send_ref)], sems)
    blocks, rhs, order = right_ref.shape
    total = inverse_ref.shape[1]
    halos = (halo0, halo1, halo2, halo3)
    halo = send_ref.shape[0]
    coarse = coarse_parts(arrived_ref[...], [inverse_ref[...]] + [ref[:, :total] for ref in halos])
    for b in range(blocks):
        update = local_ref[b] + jnp.dot(coarse[0], basis_ref[b], preferred_element_type=F32)
        update_ref[b] = update
        extended[b] = update.astype(BF)
    for q, (number, odd) in enumerate(SWAPS):
        _, slot, valid = swap_ends(number, odd)
        for m in range(halo):
            basis = halos[q][:, total + m * order : total + (m + 1) * order]
            start = total + (halo + m) * order
            local = halos[q][:, start : start + order].astype(F32)
            update = local + jnp.dot(coarse[1 + q], basis, preferred_element_type=F32)
            update_ref[blocks + halo * q + m] = update
            extended[blocks + halo * slot + m] = jnp.where(valid, update, 0.0).astype(BF)
    for copy in copies:
        copy.wait()
    upper = lower = jnp.zeros((rhs, order), F32)
    images = []
    for b in range(blocks):
        image = image_block(b, extended, tiles_ref, cols_ref)
        image_ref[b] = image
        images.append(image)
        upper += right_ref[b] * image
        lower += image * image
    row = sums_row(upper, lower)
    high, low = split(row)
    lane = lax.broadcasted_iota(jnp.int32, (1, LANES), 1)
    row = jnp.where(lane < 64, high.astype(F32), low.astype(F32))
    whole = jnp.concatenate([restrict_slot(images, basis_ref), jnp.broadcast_to(row, (SLOT, LANES))], axis=0)
    slot_ref[...] = jnp.broadcast_to(whole.astype(BF)[None], slot_ref.shape)
    leaving = fetch([(slot_ref, slot_hbm)], out_sems)
    for b in range(blocks):
        next_local_ref[b] = local_product(images[b], block_inverse_ref[b])
    for q, ((number, odd), out_hbm) in enumerate(zip(SWAPS, (out0, out1, out2, out3))):
        send, _, _ = swap_ends(number, odd)
        for m in range(halo):
            out_ref[q, :, m * order : (m + 1) * order] = next_local_ref[send_ref[m, send]].astype(BF)
        leaving += fetch([(out_ref.at[q], out_hbm)], out_sems.at[pl.ds(1 + q, 1)])
    for copy in leaving:
        copy.wait()


def second_kernel(
    cols_hbm, arrived_ref, inverse_ref, halo0, halo1, halo2, halo3, next0, next1, next2, next3,
    basis_ref, local_ref, update_ref, image_ref, right_ref, tiles_ref,
    slot_ref, scaled_ref, second_ref, residual_ref, image2_ref,
    cols_ref, extended, sems,
):
    (copy,) = fetch([(cols_hbm, cols_ref)], sems)
    blocks, rhs, order = right_ref.shape
    total = inverse_ref.shape[1]
    halos, nexts = (halo0, halo1, halo2, halo3), (next0, next1, next2, next3)
    halo = next0.shape[1] // order
    arrived = arrived_ref[...].astype(F32)
    coarse = coarse_parts(arrived[:, :SLOT], [inverse_ref[...]] + [ref[:, :total] for ref in halos])
    sums = jnp.sum(arrived[:, SLOT:], axis=0)
    turned = jnp.concatenate([sums] * (LANES // SLOT), axis=0).T
    weight = (turned[:32] + turned[64:96]) / (turned[32:64] + turned[96:] + 1e-6)
    for b in range(blocks):
        change = local_ref[b] + jnp.dot(coarse[0], basis_ref[b], preferred_element_type=F32)
        update = update_ref[b]
        second = update - weight * change
        scaled_ref[b] = weight * update
        second_ref[b] = second
        extended[b] = second.astype(BF)
    for q, (number, odd) in enumerate(SWAPS):
        _, slot, valid = swap_ends(number, odd)
        for m in range(halo):
            basis = halos[q][:, total + m * order : total + (m + 1) * order]
            local = nexts[q][:, m * order : (m + 1) * order].astype(F32)
            change = local + jnp.dot(coarse[1 + q], basis, preferred_element_type=F32)
            second = update_ref[blocks + halo * q + m] - weight * change
            extended[blocks + halo * slot + m] = jnp.where(valid, second, 0.0).astype(BF)
    copy.wait()
    upper = lower = jnp.zeros((rhs, order), F32)
    for b in range(blocks):
        residual = right_ref[b] - weight * image_ref[b]
        residual_ref[b] = residual
        image = image_block(b, extended, tiles_ref, cols_ref)
        image2_ref[b] = image
        upper += residual * image
        lower += image * image
    slot_ref[...] = jnp.broadcast_to(sums_row(upper, lower)[None], slot_ref.shape)


def last_kernel(arrived_ref, scaled_ref, second_ref, residual_ref, image_ref, solution_ref, out_ref):
    sums = jnp.sum(arrived_ref[...], axis=0)
    turned = jnp.broadcast_to(sums, (LANES, LANES)).T
    weight = turned[:32] / (turned[32:64] + 1e-6)
    for b in range(scaled_ref.shape[0]):
        solution_ref[b] = scaled_ref[b] + weight * second_ref[b]
        out_ref[b] = residual_ref[b] - weight * image_ref[b]


def call(kernel, inputs, places, outputs, scratch=()):
    kinds = {"v": pltpu.VMEM, "h": pltpu.HBM}
    into, out = places.split(">")
    inputs = [pltpu.with_memory_space_constraint(x, pltpu.HBM) if p == "h" else x for x, p in zip(inputs, into)]
    return pl.pallas_call(
        kernel,
        out_shape=[
            pltpu.HBM(shape, dtype) if p == "h" else jax.ShapeDtypeStruct(shape, dtype)
            for (shape, dtype), p in zip(outputs, out)
        ],
        in_specs=[pl.BlockSpec(memory_space=kinds[p]) for p in into],
        out_specs=[pl.BlockSpec(memory_space=kinds[p]) for p in out],
        scratch_shapes=scratch,
        compiler_params=pltpu.CompilerParams(vmem_limit_bytes=32 * 1024 * 1024),
        name=kernel.__name__,
    )(*inputs)


def exchange(slots):
    return lax.all_to_all(slots, AXES, 0, 0, tiled=True)


def body(right_sides, tiles, tile_cols, send_rows, block_inverse, coarse_basis, coarse_inverse):
    blocks, rhs, order = right_sides.shape
    rows, total = coarse_inverse.shape
    halo = send_rows.shape[1]
    count = lax.axis_size("sx") * lax.axis_size("sy")
    field = (right_sides.shape, F32)
    cols = pltpu.SMEM(tile_cols.shape, jnp.int32)
    sends = pltpu.SMEM((halo, send_rows.shape[0]), jnp.int32)
    turned_sends = send_rows.T
    extended = pltpu.VMEM((blocks + 4 * halo, rhs, order), BF)

    def sems(number):
        return pltpu.SemaphoreType.DMA((number,))

    def swapped(values):
        return [swap(value, AXES[number], odd) for value, (number, odd) in zip(values, SWAPS)]

    slots, right, inverses, basis, coarse_rows, local, *halos = call(
        start_kernel,
        (turned_sends, right_sides, block_inverse, coarse_basis, coarse_inverse),
        "hhhhh>hvvvvvhhhh",
        [
            ((count, SLOT, LANES), BF),
            field,
            (block_inverse.shape, BF),
            (coarse_basis.shape, BF),
            (coarse_inverse.shape, BF),
            field,
        ]
        + [((rhs, total + 2 * halo * order), BF)] * 4,
        (
            pltpu.VMEM((count, SLOT, LANES), BF),
            pltpu.VMEM((4, rhs, total + 2 * halo * order), BF),
            sends,
            pltpu.VMEM(coarse_inverse.shape, F32),
            sems(5),
            sems(5),
        ),
    )
    halos = swapped(halos)
    arrived = exchange(slots)
    (blocks_of_a,) = call(load_kernel, (slots, tiles), "hh>v", [(tiles.shape, BF)], (sems(blocks),))
    slots, update, image, local, *nexts = call(
        first_kernel,
        (tile_cols, turned_sends, arrived, coarse_rows, *halos, inverses, basis, local, right, blocks_of_a),
        "hhvvvvvvvvvvv>hvvvhhhh",
        [((count, 2 * SLOT, LANES), BF), ((blocks + 4 * halo, rhs, order), F32), field, field]
        + [((rhs, halo * order), BF)] * 4,
        (
            pltpu.VMEM((count, 2 * SLOT, LANES), BF),
            pltpu.VMEM((4, rhs, halo * order), BF),
            cols,
            sends,
            extended,
            sems(2),
            sems(5),
        ),
    )
    nexts = swapped(nexts)
    arrived = exchange(slots)
    slots, scaled, second, residual, image = call(
        second_kernel,
        (tile_cols, arrived, coarse_rows, *halos, *nexts, basis, local, update, image, right, blocks_of_a),
        "hvvvvvvvvvvvvvvvv>vvvvv",
        [((count, 1, LANES), F32)] + [field] * 4,
        (cols, extended, sems(1)),
    )
    return tuple(call(last_kernel, (exchange(slots), scaled, second, residual, image), "vvvvv>vv", [field] * 2))


def solution(mesh):
    block3 = P(AXES, None, None)
    placed = (block3, P(AXES, None, None, None), P(AXES, None), P(AXES, None), block3, block3, P(AXES, None))
    return jax.shard_map(body, mesh=mesh, in_specs=placed, out_specs=(block3, block3), check_vma=False)
```

```python
import functools

import jax
import jax.numpy as jnp
from jax import lax
from jax.experimental import pallas as pl
from jax.experimental.pallas import tpu as pltpu
from jax.sharding import PartitionSpec as P

AXES = ("sx", "sy")
BF = jnp.bfloat16
F32 = jnp.float32
NT = (((1,), (1,)), ((), ()))
LANES = 128
SLOT = 8
SWAPS = ((1, True), (0, True), (1, False), (0, False))
EARLY = 1, 0


def swap(value, number, odd):
    counts = [lax.axis_size(axis) for axis in AXES]
    pairs = []
    for device in range(counts[0] * counts[1]):
        place = list(divmod(device, counts[1]))
        other = place[number] + (1 if (place[number] % 2 == 0) != odd else -1)
        if 0 <= other < counts[number]:
            place[number] = other
        else:
            place[1 - number] ^= 2 if number == 0 and counts[1] % 4 == 0 else 1
        pairs.append((device, place[0] * counts[1] + place[1]))
    return lax.ppermute(value, AXES, pairs)


def swap_ends(number, odd):
    axis = AXES[number]
    place, count = lax.axis_index(axis), lax.axis_size(axis)
    up = (lax.rem(place, 2) == 0) != odd
    send = 2 * number + jnp.where(up, 0, 1)
    slot = 2 * number + jnp.where(up, 1, 0)
    valid = jnp.where(up, place < count - 1, place > 0)
    return send, slot, valid


def split(value):
    high = value.astype(BF)
    return high, (value - high.astype(F32)).astype(BF)


def restrict_slot(vectors, basis_ref):
    left, right = [], []
    for b, vector in enumerate(vectors):
        for part in split(vector):
            left.append(basis_ref[b])
            right.append(jnp.concatenate([part] * 4, axis=0))
    full = lax.dot_general(
        jnp.concatenate(left, axis=1), jnp.concatenate(right, axis=1), NT, preferred_element_type=F32
    )
    group = lax.broadcasted_iota(jnp.int32, (SLOT, LANES), 1) // 32
    slot = full[:SLOT]
    for j in range(1, 4):
        slot = jnp.where(group == j, full[SLOT * j : SLOT * (j + 1)], slot)
    return slot


def coarse_parts(arrived, inverses):
    count = arrived.shape[0]
    lane = lax.broadcasted_iota(jnp.int32, (1, 4, SLOT, LANES), 3) // 32
    part = lax.broadcasted_iota(jnp.int32, (1, 4, SLOT, LANES), 1)
    spread_out = jnp.where(lane == part, arrived[:, None].astype(F32), 0.0)
    column = spread_out.reshape(count * 4 * SLOT, LANES).astype(BF)
    product = jnp.dot(inverses, column, preferred_element_type=F32)
    parts = []
    for s in range(inverses.shape[0] // 32):
        turned = product[32 * s : 32 * (s + 1)].T
        parts.append((turned[:32] + turned[32:64] + turned[64:96] + turned[96:]).astype(BF))
    return parts


def local_product(vector, inverse):
    rows = vector.shape[0]
    both = lax.dot_general(jnp.concatenate(split(vector), axis=0), inverse, NT, preferred_element_type=F32)
    return both[:rows] + both[rows:]


def image_block(b, extended, tiles, cols_ref):
    vectors = [extended[b]] + [extended[cols_ref[b, t]] for t in range(tiles.shape[1] - 1)]
    blocks = [tiles[b, t] for t in range(tiles.shape[1])]
    return lax.dot_general(
        jnp.concatenate(vectors, axis=1), jnp.concatenate(blocks, axis=1), NT, preferred_element_type=F32
    )


def sums_row(upper, lower):
    return jnp.sum(jnp.concatenate([upper, lower, upper, lower], axis=0).T, axis=0, keepdims=True)


def fetch(pairs, sems):
    copies = [pltpu.make_async_copy(source, target, sems.at[k]) for k, (source, target) in enumerate(pairs)]
    for copy in copies:
        copy.start()
    return copies


def start_kernel(
    send_hbm, right_hbm, block_inverse_hbm, basis_hbm, inverse_hbm,
    slot_hbm, right_ref, block_inverse_ref, basis_ref, inverse_ref, local_ref, out0, out1, out2, out3,
    slot_ref, out_ref, send_ref, wide, sems, out_sems,
):
    copies = fetch(
        [
            (right_hbm, right_ref),
            (basis_hbm, basis_ref),
            (block_inverse_hbm, block_inverse_ref),
            (inverse_hbm, wide),
            (send_hbm, send_ref),
        ],
        sems,
    )
    blocks, rhs, order = right_ref.shape
    halo = send_ref.shape[0]
    total = wide.shape[1]
    for copy in copies[:2]:
        copy.wait()
    vectors = [right_ref[b] for b in range(blocks)]
    slot_ref[...] = jnp.broadcast_to(restrict_slot(vectors, basis_ref).astype(BF)[None], slot_ref.shape)
    leaving = fetch([(slot_ref, slot_hbm)], out_sems)
    copies[2].wait()
    for b in range(blocks):
        local_ref[b] = local_product(right_ref[b], block_inverse_ref[b])
    copies[3].wait()
    inverse = wide[...].astype(BF)
    inverse_ref[...] = inverse
    copies[4].wait()
    for q, ((number, odd), out_hbm) in enumerate(zip(SWAPS, (out0, out1, out2, out3))):
        send, _, _ = swap_ends(number, odd)
        out_ref[q, :, :total] = inverse
        for m in range(halo):
            row = send_ref[m, send]
            out_ref[q, :, total + m * order : total + (m + 1) * order] = basis_ref[row]
            start = total + (halo + m) * order
            out_ref[q, :, start : start + order] = local_ref[row].astype(BF)
        leaving += fetch([(out_ref.at[q], out_hbm)], out_sems.at[pl.ds(1 + q, 1)])
    for copy in leaving:
        copy.wait()


def gather_kernel(inverse_ref, basis_ref, tiles_hbm, *refs):
    halos, (inverses_ref, bases_ref, locals_ref, tiles_ref, sems, tile_sems) = refs[:-6], refs[-6:]
    rows, total = inverse_ref.shape
    blocks, _, order = basis_ref.shape
    pairs = []
    for q, ref in enumerate(halos):
        pairs.append((ref.at[:, pl.ds(0, total)], inverses_ref.at[pl.ds(rows * (1 + q), rows)]))
        halo = (ref.shape[1] - total) // (2 * order)
        for m in range(halo):
            at = total + m * order
            pairs.append((ref.at[:, pl.ds(at, order)], bases_ref.at[blocks + halo * q + m]))
            pairs.append((ref.at[:, pl.ds(at + halo * order, order)], locals_ref.at[halo * q + m]))
    copies = fetch(pairs, sems)
    copies += fetch([(tiles_hbm.at[b], tiles_ref.at[b]) for b in range(tiles_ref.shape[0])], tile_sems)
    inverses_ref[:rows] = inverse_ref[...]
    bases_ref[:blocks] = basis_ref[...]
    for copy in copies:
        copy.wait()


def all_inverses(inverses_ref, late):
    total = inverses_ref.shape[1]
    return jnp.concatenate([inverses_ref[...]] + [ref[:, :total] for ref in late], axis=0)


def basis_block(k, bases_ref, late, total, halo):
    if k < bases_ref.shape[0]:
        return bases_ref[k]
    q, m = divmod(k - bases_ref.shape[0], halo)
    order = bases_ref.shape[2]
    return late[q][:, total + m * order : total + (m + 1) * order]


def pack(extended, k, value, blocks, halo):
    if k < blocks:
        extended[k] = value.astype(BF)
    else:
        q, m = divmod(k - blocks, halo)
        _, slot, valid = swap_ends(*SWAPS[q])
        extended[blocks + halo * slot + m] = jnp.where(valid, value, 0.0).astype(BF)


def owner(k, blocks, halo):
    return 0 if k < blocks else 1 + (k - blocks) // halo


def first_kernel(
    cols_hbm, send_hbm, arrived_ref, inverses_ref, bases_ref, local_ref, locals_ref, block_inverse_ref, right_ref,
    tiles_ref, *refs,
):
    late, refs = refs[: 4 - EARLY[0]], refs[4 - EARLY[0] :]
    slot_hbm, update_ref, image_ref, out0, out1, out2, out3 = refs[:7]
    slot_ref, out_ref, cols_ref, send_ref, extended, sems, out_sems = refs[7:]
    copies = fetch([(cols_hbm, cols_ref), (send_hbm, send_ref)], sems)
    blocks, rhs, order = right_ref.shape
    halo = send_ref.shape[0]
    total = inverses_ref.shape[1]
    coarse = coarse_parts(arrived_ref[...], all_inverses(inverses_ref, late))
    early = blocks + halo * EARLY[0]
    for k in range(update_ref.shape[0]):
        basis = basis_block(k, bases_ref, late, total, halo)
        if k < blocks:
            local = local_ref[k]
        elif k < early:
            local = locals_ref[k - blocks].astype(F32)
        else:
            q, m = divmod(k - early, halo)
            at = total + (halo + m) * order
            local = late[q][:, at : at + order].astype(F32)
        update = local + jnp.dot(coarse[owner(k, blocks, halo)], basis, preferred_element_type=F32)
        update_ref[k] = update
        pack(extended, k, update, blocks, halo)
    for copy in copies:
        copy.wait()
    upper = lower = jnp.zeros((rhs, order), F32)
    images = []
    for b in range(blocks):
        image = image_block(b, extended, tiles_ref, cols_ref)
        image_ref[b] = image
        images.append(image)
        upper += right_ref[b] * image
        lower += image * image
    row = sums_row(upper, lower)
    high, low = split(row)
    lane = lax.broadcasted_iota(jnp.int32, (1, LANES), 1)
    row = jnp.where(lane < 64, high.astype(F32), low.astype(F32))
    whole = jnp.concatenate([restrict_slot(images, bases_ref), jnp.broadcast_to(row, (SLOT, LANES))], axis=0)
    slot_ref[...] = jnp.broadcast_to(whole.astype(BF)[None], slot_ref.shape)
    leaving = fetch([(slot_ref, slot_hbm)], out_sems)
    for q, ((number, odd), out_hbm) in enumerate(zip(SWAPS, (out0, out1, out2, out3))):
        send, _, _ = swap_ends(number, odd)
        for m in range(halo):
            row = send_ref[m, send]
            local = local_product(image_ref[row], block_inverse_ref[row])
            out_ref[q, :, m * order : (m + 1) * order] = local.astype(BF)
        leaving += fetch([(out_ref.at[q], out_hbm)], out_sems.at[pl.ds(1 + q, 1)])
    for copy in leaving:
        copy.wait()


def local_kernel(image_ref, block_inverse_ref, *refs):
    blocks, _, order = image_ref.shape
    local_ref = refs[-1]
    for b in range(blocks):
        local_ref[b] = local_product(image_ref[b], block_inverse_ref[b])
    for q, ref in enumerate(refs[:-1]):
        halo = ref.shape[1] // order
        for m in range(halo):
            local_ref[blocks + halo * q + m] = ref[:, m * order : (m + 1) * order].astype(F32)


def second_kernel(
    cols_hbm, arrived_ref, inverses_ref, bases_ref, local_ref, update_ref, image_ref, right_ref, tiles_ref, *refs,
):
    late, refs = refs[: 4 - EARLY[0]], refs[4 - EARLY[0] :]
    nexts, refs = refs[: 4 - EARLY[1]], refs[4 - EARLY[1] :]
    slot_ref, scaled_ref, second_ref, residual_ref, image2_ref, cols_ref, extended, sems = refs
    (copy,) = fetch([(cols_hbm, cols_ref)], sems)
    blocks, rhs, order = right_ref.shape
    halo = (update_ref.shape[0] - blocks) // 4
    total = inverses_ref.shape[1]
    arrived = arrived_ref[...].astype(F32)
    coarse = coarse_parts(arrived[:, :SLOT], all_inverses(inverses_ref, late))
    sums = jnp.sum(arrived[:, SLOT:], axis=0)
    turned = jnp.concatenate([sums] * (LANES // SLOT), axis=0).T
    weight = (turned[:32] + turned[64:96]) / (turned[32:64] + turned[96:] + 1e-6)
    for k in range(update_ref.shape[0]):
        basis = basis_block(k, bases_ref, late, total, halo)
        if k < local_ref.shape[0]:
            local = local_ref[k]
        else:
            q, m = divmod(k - local_ref.shape[0], halo)
            local = nexts[q][:, m * order : (m + 1) * order].astype(F32)
        update = update_ref[k]
        spread = jnp.dot(coarse[owner(k, blocks, halo)], basis, preferred_element_type=F32)
        second = update - weight * (local + spread)
        if k < blocks:
            scaled_ref[k] = weight * update
            second_ref[k] = second
        pack(extended, k, second, blocks, halo)
    copy.wait()
    upper = lower = jnp.zeros((rhs, order), F32)
    for b in range(blocks):
        residual = right_ref[b] - weight * image_ref[b]
        residual_ref[b] = residual
        image = image_block(b, extended, tiles_ref, cols_ref)
        image2_ref[b] = image
        upper += residual * image
        lower += image * image
    slot_ref[...] = jnp.broadcast_to(sums_row(upper, lower)[None], slot_ref.shape)


def last_kernel(arrived_ref, scaled_ref, second_ref, residual_ref, image_ref, solution_ref, out_ref):
    sums = jnp.sum(arrived_ref[...], axis=0)
    turned = jnp.broadcast_to(sums, (LANES, LANES)).T
    weight = turned[:32] / (turned[32:64] + 1e-6)
    for b in range(scaled_ref.shape[0]):
        solution_ref[b] = scaled_ref[b] + weight * second_ref[b]
        out_ref[b] = residual_ref[b] - weight * image_ref[b]


def call(kernel, inputs, places, outputs, scratch=(), flops=None):
    kinds = {"v": pltpu.VMEM, "h": pltpu.HBM}
    into, out = places.split(">")
    inputs = [pltpu.with_memory_space_constraint(x, pltpu.HBM) if p == "h" else x for x, p in zip(inputs, into)]
    return pl.pallas_call(
        kernel,
        out_shape=[
            pltpu.HBM(shape, dtype) if p == "h" else jax.ShapeDtypeStruct(shape, dtype)
            for (shape, dtype), p in zip(outputs, out)
        ],
        in_specs=[pl.BlockSpec(memory_space=kinds[p]) for p in into],
        out_specs=[pl.BlockSpec(memory_space=kinds[p]) for p in out],
        scratch_shapes=scratch,
        compiler_params=pltpu.CompilerParams(vmem_limit_bytes=32 * 1024 * 1024),
        cost_estimate=flops and pl.CostEstimate(flops=flops, bytes_accessed=0, transcendentals=0),
        name=kernel.__name__,
    )(*inputs)


def exchange(slots):
    return lax.all_to_all(slots, AXES, 0, 0, tiled=True)


def body(right_sides, tiles, tile_cols, send_rows, block_inverse, coarse_basis, coarse_inverse):
    blocks, rhs, order = right_sides.shape
    rows, total = coarse_inverse.shape
    halo = send_rows.shape[1]
    count = lax.axis_size("sx") * lax.axis_size("sy")
    field = (right_sides.shape, F32)
    cols = pltpu.SMEM(tile_cols.shape, jnp.int32)
    sends = pltpu.SMEM((halo, send_rows.shape[0]), jnp.int32)
    turned_sends = send_rows.T
    extended = pltpu.VMEM((blocks + 4 * halo, rhs, order), BF)

    def sems(number):
        return pltpu.SemaphoreType.DMA((number,))

    def swapped(values):
        return [swap(value, number, odd) for value, (number, odd) in zip(values, SWAPS)]

    slots, right, inverses, basis, coarse_rows, local, *halos = call(
        start_kernel,
        (turned_sends, right_sides, block_inverse, coarse_basis, coarse_inverse),
        "hhhhh>hvvvvvhhhh",
        [
            ((count, SLOT, LANES), BF),
            field,
            (block_inverse.shape, BF),
            (coarse_basis.shape, BF),
            (coarse_inverse.shape, BF),
            field,
        ]
        + [((rhs, total + 2 * halo * order), BF)] * 4,
        (
            pltpu.VMEM((count, SLOT, LANES), BF),
            pltpu.VMEM((4, rhs, total + 2 * halo * order), BF),
            sends,
            pltpu.VMEM(coarse_inverse.shape, F32),
            sems(5),
            sems(5),
        ),
    )
    halos = swapped(halos)
    early, late = halos[: EARLY[0]], halos[EARLY[0] :]
    arrived = exchange(slots)
    reach = blocks + halo * EARLY[0]
    coarse_rows, bases, locals_, blocks_of_a = call(
        gather_kernel,
        (coarse_rows, basis, tiles, *early),
        "vvh" + "h" * len(early) + ">vvvv",
        [
            (((1 + EARLY[0]) * rows, total), BF),
            ((reach,) + coarse_basis.shape[1:], BF),
            ((max(reach - blocks, 1), rhs, order), BF),
            (tiles.shape, BF),
        ],
        (sems(max(1, (1 + 2 * halo) * EARLY[0])), sems(blocks)),
        flops=10**11 if EARLY[0] else None,
    )
    slots, update, image, *nexts = call(
        first_kernel,
        (tile_cols, turned_sends, arrived, coarse_rows, bases, local, locals_, inverses, right, blocks_of_a, *late),
        "hhvvvvvvvv" + "v" * len(late) + ">hvvhhhh",
        [((count, 2 * SLOT, LANES), BF), ((blocks + 4 * halo, rhs, order), F32), field]
        + [((rhs, halo * order), BF)] * 4,
        (
            pltpu.VMEM((count, 2 * SLOT, LANES), BF),
            pltpu.VMEM((4, rhs, halo * order), BF),
            cols,
            sends,
            extended,
            sems(2),
            sems(5),
        ),
    )
    nexts = swapped(nexts)
    soon, nexts = nexts[: EARLY[1]], nexts[EARLY[1] :]
    arrived = exchange(slots)
    (local,) = call(
        local_kernel,
        (image, inverses, *soon),
        "vv" + "v" * len(soon) + ">v",
        [((blocks + halo * EARLY[1], rhs, order), F32)],
        flops=10**11 if EARLY[1] else None,
    )
    slots, scaled, second, residual, image = call(
        second_kernel,
        (tile_cols, arrived, coarse_rows, bases, local, update, image, right, blocks_of_a, *late, *nexts),
        "hvvvvvvvv" + "v" * (len(late) + len(nexts)) + ">vvvvv",
        [((count, 1, LANES), F32)] + [field] * 4,
        (cols, extended, sems(1)),
    )
    return tuple(call(last_kernel, (exchange(slots), scaled, second, residual, image), "vvvvv>vv", [field] * 2))


def solution(mesh):
    block3 = P(AXES, None, None)
    placed = (block3, P(AXES, None, None, None), P(AXES, None), P(AXES, None), block3, block3, P(AXES, None))
    return jax.shard_map(body, mesh=mesh, in_specs=placed, out_specs=(block3, block3), check_vma=False)
```

```python
import functools

import jax
import jax.numpy as jnp
from jax import lax
from jax.experimental import pallas as pl
from jax.experimental.pallas import tpu as pltpu
from jax.sharding import PartitionSpec as P

AXES = ("sx", "sy")
BF = jnp.bfloat16
F32 = jnp.float32
NT = (((1,), (1,)), ((), ()))
LANES = 128
SLOT = 8
SWAPS = ((1, True), (0, True), (1, False), (0, False))
EARLY = 1, 0


def swap(value, number, odd):
    counts = [lax.axis_size(axis) for axis in AXES]
    pairs = []
    for device in range(counts[0] * counts[1]):
        place = list(divmod(device, counts[1]))
        other = place[number] + (1 if (place[number] % 2 == 0) != odd else -1)
        if 0 <= other < counts[number]:
            place[number] = other
        else:
            place[1 - number] ^= 2 if number == 0 and counts[1] % 4 == 0 else 1
        pairs.append((device, place[0] * counts[1] + place[1]))
    return lax.ppermute(value, AXES, pairs)


def swap_ends(number, odd):
    axis = AXES[number]
    place, count = lax.axis_index(axis), lax.axis_size(axis)
    up = (lax.rem(place, 2) == 0) != odd
    send = 2 * number + jnp.where(up, 0, 1)
    slot = 2 * number + jnp.where(up, 1, 0)
    valid = jnp.where(up, place < count - 1, place > 0)
    return send, slot, valid


def split(value):
    high = value.astype(BF)
    return high, (value - high.astype(F32)).astype(BF)


def restrict_slot(vectors, basis_ref):
    left, right = [], []
    for b, vector in enumerate(vectors):
        for part in split(vector):
            left.append(basis_ref[b])
            right.append(jnp.concatenate([part] * 4, axis=0))
    full = lax.dot_general(
        jnp.concatenate(left, axis=1), jnp.concatenate(right, axis=1), NT, preferred_element_type=F32
    )
    group = lax.broadcasted_iota(jnp.int32, (SLOT, LANES), 1) // 32
    slot = full[:SLOT]
    for j in range(1, 4):
        slot = jnp.where(group == j, full[SLOT * j : SLOT * (j + 1)], slot)
    return slot


def coarse_parts(arrived, inverses):
    count = arrived.shape[0]
    lane = lax.broadcasted_iota(jnp.int32, (1, 4, SLOT, LANES), 3) // 32
    part = lax.broadcasted_iota(jnp.int32, (1, 4, SLOT, LANES), 1)
    spread_out = jnp.where(lane == part, arrived[:, None].astype(F32), 0.0)
    column = spread_out.reshape(count * 4 * SLOT, LANES).astype(BF)
    product = jnp.dot(inverses, column, preferred_element_type=F32)
    parts = []
    for s in range(inverses.shape[0] // 32):
        turned = product[32 * s : 32 * (s + 1)].T
        parts.append((turned[:32] + turned[32:64] + turned[64:96] + turned[96:]).astype(BF))
    return parts


def local_product(vector, inverse):
    rows = vector.shape[0]
    both = lax.dot_general(jnp.concatenate(split(vector), axis=0), inverse, NT, preferred_element_type=F32)
    return both[:rows] + both[rows:]


def image_block(b, extended, tiles, cols_ref):
    vectors = [extended[b]] + [extended[cols_ref[b, t]] for t in range(tiles.shape[1] - 1)]
    blocks = [tiles[b, t] for t in range(tiles.shape[1])]
    return lax.dot_general(
        jnp.concatenate(vectors, axis=1), jnp.concatenate(blocks, axis=1), NT, preferred_element_type=F32
    )


def sums_row(upper, lower):
    return jnp.sum(jnp.concatenate([upper, lower, upper, lower], axis=0).T, axis=0, keepdims=True)


def fetch(pairs, sems):
    copies = [pltpu.make_async_copy(source, target, sems.at[k]) for k, (source, target) in enumerate(pairs)]
    for copy in copies:
        copy.start()
    return copies


def start_kernel(
    send_hbm, right_hbm, block_inverse_hbm, basis_hbm, inverse_hbm,
    slot_hbm, right_ref, block_inverse_ref, basis_ref, inverse_ref, out0, out1, out2, out3,
    slot_ref, out_ref, send_ref, wide, sems, out_sems,
):
    copies = fetch(
        [
            (right_hbm, right_ref),
            (basis_hbm, basis_ref),
            (block_inverse_hbm, block_inverse_ref),
            (inverse_hbm, wide),
            (send_hbm, send_ref),
        ],
        sems,
    )
    blocks, rhs, order = right_ref.shape
    halo = send_ref.shape[0]
    total = wide.shape[1]
    for copy in copies[:2]:
        copy.wait()
    vectors = [right_ref[b] for b in range(blocks)]
    slot_ref[...] = jnp.broadcast_to(restrict_slot(vectors, basis_ref).astype(BF)[None], slot_ref.shape)
    leaving = fetch([(slot_ref, slot_hbm)], out_sems)
    copies[3].wait()
    inverse = wide[...].astype(BF)
    inverse_ref[...] = inverse
    copies[2].wait()
    copies[4].wait()
    for q, ((number, odd), out_hbm) in enumerate(zip(SWAPS, (out0, out1, out2, out3))):
        send, _, _ = swap_ends(number, odd)
        out_ref[q, :, :total] = inverse
        for m in range(halo):
            row = send_ref[m, send]
            out_ref[q, :, total + m * order : total + (m + 1) * order] = basis_ref[row]
            start = total + (halo + m) * order
            local = local_product(right_ref[row], block_inverse_ref[row])
            out_ref[q, :, start : start + order] = local.astype(BF)
        leaving += fetch([(out_ref.at[q], out_hbm)], out_sems.at[pl.ds(1 + q, 1)])
    for copy in leaving:
        copy.wait()


def gather_kernel(inverse_ref, basis_ref, right_ref, block_inverse_ref, tiles_hbm, cols_hbm, send_hbm, *refs):
    halos, refs = refs[: EARLY[0]], refs[EARLY[0] :]
    inverses_ref, bases_ref, locals_ref, tiles_ref, cols_ref, send_ref, local_ref, sems, tile_sems = refs
    rows, total = inverse_ref.shape
    blocks, _, order = basis_ref.shape
    copies = fetch([(cols_hbm, cols_ref), (send_hbm, send_ref)], sems)
    copies += fetch([(tiles_hbm.at[b], tiles_ref.at[b]) for b in range(tiles_ref.shape[0])], tile_sems)
    for b in range(blocks):
        local_ref[b] = local_product(right_ref[b], block_inverse_ref[b])
    inverses_ref[:rows] = inverse_ref[...]
    bases_ref[:blocks] = basis_ref[...]
    for q, ref in enumerate(halos):
        inverses_ref[rows * (1 + q) : rows * (2 + q)] = ref[:, :total]
        halo = (ref.shape[1] - total) // (2 * order)
        for m in range(halo):
            at = total + m * order
            bases_ref[blocks + halo * q + m] = ref[:, at : at + order]
            at += halo * order
            locals_ref[halo * q + m] = ref[:, at : at + order]
    for copy in copies:
        copy.wait()


def all_inverses(inverses_ref, late):
    total = inverses_ref.shape[1]
    return jnp.concatenate([inverses_ref[...]] + [ref[:, :total] for ref in late], axis=0)


def basis_block(k, bases_ref, late, total, halo):
    if k < bases_ref.shape[0]:
        return bases_ref[k]
    q, m = divmod(k - bases_ref.shape[0], halo)
    order = bases_ref.shape[2]
    return late[q][:, total + m * order : total + (m + 1) * order]


def pack(extended, k, value, blocks, halo):
    if k < blocks:
        extended[k] = value.astype(BF)
    else:
        q, m = divmod(k - blocks, halo)
        _, slot, valid = swap_ends(*SWAPS[q])
        extended[blocks + halo * slot + m] = jnp.where(valid, value, 0.0).astype(BF)


def owner(k, blocks, halo):
    return 0 if k < blocks else 1 + (k - blocks) // halo


def first_kernel(
    cols_vmem, send_vmem, arrived_ref, inverses_ref, bases_ref, local_ref, locals_ref, block_inverse_ref, right_ref,
    tiles_ref, *refs,
):
    late, refs = refs[: 4 - EARLY[0]], refs[4 - EARLY[0] :]
    slot_hbm, update_ref, image_ref, out0, out1, out2, out3 = refs[:7]
    slot_ref, out_ref, cols_ref, send_ref, extended, sems, out_sems = refs[7:]
    copies = fetch([(cols_vmem, cols_ref), (send_vmem, send_ref)], sems)
    blocks, rhs, order = right_ref.shape
    halo = send_ref.shape[0]
    total = inverses_ref.shape[1]
    coarse = coarse_parts(arrived_ref[...], all_inverses(inverses_ref, late))
    early = blocks + halo * EARLY[0]
    for k in range(update_ref.shape[0]):
        basis = basis_block(k, bases_ref, late, total, halo)
        if k < blocks:
            local = local_ref[k]
        elif k < early:
            local = locals_ref[k - blocks].astype(F32)
        else:
            q, m = divmod(k - early, halo)
            at = total + (halo + m) * order
            local = late[q][:, at : at + order].astype(F32)
        update = local + jnp.dot(coarse[owner(k, blocks, halo)], basis, preferred_element_type=F32)
        update_ref[k] = update
        pack(extended, k, update, blocks, halo)
    for copy in copies:
        copy.wait()
    upper = lower = jnp.zeros((rhs, order), F32)
    images = []
    for b in range(blocks):
        image = image_block(b, extended, tiles_ref, cols_ref)
        image_ref[b] = image
        images.append(image)
        upper += right_ref[b] * image
        lower += image * image
    row = sums_row(upper, lower)
    high, low = split(row)
    lane = lax.broadcasted_iota(jnp.int32, (1, LANES), 1)
    row = jnp.where(lane < 64, high.astype(F32), low.astype(F32))
    slot = restrict_slot(images, bases_ref)
    half = SLOT // 2
    whole = jnp.concatenate([slot[:half], slot[half:], jnp.broadcast_to(row, (half, LANES))], axis=1)
    slot_ref[...] = jnp.broadcast_to(whole.astype(BF)[None], slot_ref.shape)
    leaving = fetch([(slot_ref, slot_hbm)], out_sems)
    for q, ((number, odd), out_hbm) in enumerate(zip(SWAPS, (out0, out1, out2, out3))):
        send, _, _ = swap_ends(number, odd)
        for m in range(halo):
            row = send_ref[m, send]
            local = local_product(image_ref[row], block_inverse_ref[row])
            out_ref[q, :, m * order : (m + 1) * order] = local.astype(BF)
        leaving += fetch([(out_ref.at[q], out_hbm)], out_sems.at[pl.ds(1 + q, 1)])
    for copy in leaving:
        copy.wait()


def local_kernel(image_ref, block_inverse_ref, *refs):
    blocks, _, order = image_ref.shape
    local_ref = refs[-1]
    for b in range(blocks):
        local_ref[b] = local_product(image_ref[b], block_inverse_ref[b])
    for q, ref in enumerate(refs[:-1]):
        halo = ref.shape[1] // order
        for m in range(halo):
            local_ref[blocks + halo * q + m] = ref[:, m * order : (m + 1) * order].astype(F32)


def second_kernel(
    cols_vmem, arrived_ref, inverses_ref, bases_ref, local_ref, update_ref, image_ref, right_ref, tiles_ref, *refs,
):
    late, refs = refs[: 4 - EARLY[0]], refs[4 - EARLY[0] :]
    nexts, refs = refs[: 4 - EARLY[1]], refs[4 - EARLY[1] :]
    slot_ref, scaled_ref, second_ref, residual_ref, image2_ref, cols_ref, extended, sems = refs
    (copy,) = fetch([(cols_vmem, cols_ref)], sems)
    blocks, rhs, order = right_ref.shape
    halo = (update_ref.shape[0] - blocks) // 4
    total = inverses_ref.shape[1]
    arrived = arrived_ref[...].astype(F32)
    restricted = jnp.concatenate([arrived[:, :, :LANES], arrived[:, :, LANES : 2 * LANES]], axis=1)
    coarse = coarse_parts(restricted, all_inverses(inverses_ref, late))
    sums = jnp.sum(arrived[:, :1, 2 * LANES :], axis=0)
    turned = jnp.broadcast_to(sums, (LANES, LANES)).T
    weight = (turned[:32] + turned[64:96]) / (turned[32:64] + turned[96:] + 1e-6)
    for k in range(update_ref.shape[0]):
        basis = basis_block(k, bases_ref, late, total, halo)
        if k < local_ref.shape[0]:
            local = local_ref[k]
        else:
            q, m = divmod(k - local_ref.shape[0], halo)
            local = nexts[q][:, m * order : (m + 1) * order].astype(F32)
        update = update_ref[k]
        spread = jnp.dot(coarse[owner(k, blocks, halo)], basis, preferred_element_type=F32)
        second = update - weight * (local + spread)
        if k < blocks:
            scaled_ref[k] = weight * update
            second_ref[k] = second
        pack(extended, k, second, blocks, halo)
    copy.wait()
    upper = lower = jnp.zeros((rhs, order), F32)
    for b in range(blocks):
        residual = right_ref[b] - weight * image_ref[b]
        residual_ref[b] = residual
        image = image_block(b, extended, tiles_ref, cols_ref)
        image2_ref[b] = image
        upper += residual * image
        lower += image * image
    slot_ref[...] = jnp.broadcast_to(sums_row(upper, lower)[None], slot_ref.shape)


def last_kernel(arrived_ref, scaled_ref, second_ref, residual_ref, image_ref, solution_ref, out_ref):
    sums = jnp.sum(arrived_ref[...], axis=0)
    turned = jnp.broadcast_to(sums, (LANES, LANES)).T
    weight = turned[:32] / (turned[32:64] + 1e-6)
    for b in range(scaled_ref.shape[0]):
        solution_ref[b] = scaled_ref[b] + weight * second_ref[b]
        out_ref[b] = residual_ref[b] - weight * image_ref[b]


def call(kernel, inputs, places, outputs, scratch=(), flops=None):
    kinds = {"v": pltpu.VMEM, "h": pltpu.HBM}
    into, out = places.split(">")
    inputs = [pltpu.with_memory_space_constraint(x, pltpu.HBM) if p == "h" else x for x, p in zip(inputs, into)]
    return pl.pallas_call(
        kernel,
        out_shape=[
            pltpu.HBM(shape, dtype) if p == "h" else jax.ShapeDtypeStruct(shape, dtype)
            for (shape, dtype), p in zip(outputs, out)
        ],
        in_specs=[pl.BlockSpec(memory_space=kinds[p]) for p in into],
        out_specs=[pl.BlockSpec(memory_space=kinds[p]) for p in out],
        scratch_shapes=scratch,
        compiler_params=pltpu.CompilerParams(vmem_limit_bytes=32 * 1024 * 1024),
        cost_estimate=flops and pl.CostEstimate(flops=flops, bytes_accessed=0, transcendentals=0),
        name=kernel.__name__,
    )(*inputs)


def exchange(slots):
    return lax.all_to_all(slots, AXES, 0, 0, tiled=True)


def body(right_sides, tiles, tile_cols, send_rows, block_inverse, coarse_basis, coarse_inverse):
    blocks, rhs, order = right_sides.shape
    rows, total = coarse_inverse.shape
    halo = send_rows.shape[1]
    count = lax.axis_size("sx") * lax.axis_size("sy")
    field = (right_sides.shape, F32)
    cols = pltpu.SMEM(tile_cols.shape, jnp.int32)
    sends = pltpu.SMEM((halo, send_rows.shape[0]), jnp.int32)
    turned_sends = send_rows.T
    extended = pltpu.VMEM((blocks + 4 * halo, rhs, order), BF)

    def sems(number):
        return pltpu.SemaphoreType.DMA((number,))

    def swapped(values):
        return [swap(value, number, odd) for value, (number, odd) in zip(values, SWAPS)]

    slots, right, inverses, basis, coarse_rows, *halos = call(
        start_kernel,
        (turned_sends, right_sides, block_inverse, coarse_basis, coarse_inverse),
        "hhhhh>hvvvvhhhh",
        [
            ((count, SLOT, LANES), BF),
            field,
            (block_inverse.shape, BF),
            (coarse_basis.shape, BF),
            (coarse_inverse.shape, BF),
        ]
        + [((rhs, total + 2 * halo * order), BF)] * 4,
        (
            pltpu.VMEM((count, SLOT, LANES), BF),
            pltpu.VMEM((4, rhs, total + 2 * halo * order), BF),
            sends,
            pltpu.VMEM(coarse_inverse.shape, F32),
            sems(5),
            sems(5),
        ),
    )
    halos = swapped(halos)
    early, late = halos[: EARLY[0]], halos[EARLY[0] :]
    arrived = exchange(slots)
    reach = blocks + halo * EARLY[0]
    coarse_rows, bases, locals_, blocks_of_a, tile_cols, turned_sends, local = call(
        gather_kernel,
        (coarse_rows, basis, right, inverses, tiles, tile_cols, turned_sends, *early),
        "vvvvhhh" + "v" * len(early) + ">vvvvvvv",
        [
            (((1 + EARLY[0]) * rows, total), BF),
            ((reach,) + coarse_basis.shape[1:], BF),
            ((max(reach - blocks, 1), rhs, order), BF),
            (tiles.shape, BF),
            (tile_cols.shape, jnp.int32),
            (turned_sends.shape, jnp.int32),
            field,
        ],
        (sems(2), sems(blocks)),
        flops=10**11 if EARLY[0] else None,
    )
    slots, update, image, *nexts = call(
        first_kernel,
        (tile_cols, turned_sends, arrived, coarse_rows, bases, local, locals_, inverses, right, blocks_of_a, *late),
        "vvvvvvvvvv" + "v" * len(late) + ">hvvhhhh",
        [((count, SLOT // 2, 3 * LANES), BF), ((blocks + 4 * halo, rhs, order), F32), field]
        + [((rhs, halo * order), BF)] * 4,
        (
            pltpu.VMEM((count, SLOT // 2, 3 * LANES), BF),
            pltpu.VMEM((4, rhs, halo * order), BF),
            cols,
            sends,
            extended,
            sems(2),
            sems(5),
        ),
    )
    nexts = swapped(nexts)
    soon, nexts = nexts[: EARLY[1]], nexts[EARLY[1] :]
    arrived = exchange(slots)
    (local,) = call(
        local_kernel,
        (image, inverses, *soon),
        "vv" + "v" * len(soon) + ">v",
        [((blocks + halo * EARLY[1], rhs, order), F32)],
        flops=10**11 if EARLY[1] else None,
    )
    slots, scaled, second, residual, image = call(
        second_kernel,
        (tile_cols, arrived, coarse_rows, bases, local, update, image, right, blocks_of_a, *late, *nexts),
        "vvvvvvvvv" + "v" * (len(late) + len(nexts)) + ">vvvvv",
        [((count, 1, LANES), F32)] + [field] * 4,
        (cols, extended, sems(1)),
    )
    return tuple(call(last_kernel, (exchange(slots), scaled, second, residual, image), "vvvvv>vv", [field] * 2))


def solution(mesh):
    block3 = P(AXES, None, None)
    placed = (block3, P(AXES, None, None, None), P(AXES, None), P(AXES, None), block3, block3, P(AXES, None))
    return jax.shard_map(body, mesh=mesh, in_specs=placed, out_specs=(block3, block3), check_vma=False)
```

```python
import functools

import jax
import jax.numpy as jnp
from jax import lax
from jax.experimental import pallas as pl
from jax.experimental.pallas import tpu as pltpu
from jax.sharding import PartitionSpec as P

AXES = ("sx", "sy")
BF = jnp.bfloat16
F32 = jnp.float32
NT = (((1,), (1,)), ((), ()))
LANES = 128
SLOT = 8
SWAPS = ((1, True), (0, True), (1, False), (0, False))
EARLY = 1, 0


def swap(value, number, odd):
    counts = [lax.axis_size(axis) for axis in AXES]
    pairs = []
    for device in range(counts[0] * counts[1]):
        place = list(divmod(device, counts[1]))
        other = place[number] + (1 if (place[number] % 2 == 0) != odd else -1)
        if 0 <= other < counts[number]:
            place[number] = other
        else:
            place[1 - number] ^= 2 if number == 0 and counts[1] % 4 == 0 else 1
        pairs.append((device, place[0] * counts[1] + place[1]))
    return lax.ppermute(value, AXES, pairs)


def swap_ends(number, odd):
    axis = AXES[number]
    place, count = lax.axis_index(axis), lax.axis_size(axis)
    up = (lax.rem(place, 2) == 0) != odd
    send = 2 * number + jnp.where(up, 0, 1)
    slot = 2 * number + jnp.where(up, 1, 0)
    valid = jnp.where(up, place < count - 1, place > 0)
    return send, slot, valid


def split(value):
    high = value.astype(BF)
    return high, (value - high.astype(F32)).astype(BF)


def restrict_slot(vectors, basis_ref):
    left, right = [], []
    for b, vector in enumerate(vectors):
        for part in split(vector):
            left.append(basis_ref[b])
            right.append(jnp.concatenate([part] * 4, axis=0))
    full = lax.dot_general(
        jnp.concatenate(left, axis=1), jnp.concatenate(right, axis=1), NT, preferred_element_type=F32
    )
    group = lax.broadcasted_iota(jnp.int32, (SLOT, LANES), 1) // 32
    slot = full[:SLOT]
    for j in range(1, 4):
        slot = jnp.where(group == j, full[SLOT * j : SLOT * (j + 1)], slot)
    return slot


def coarse_parts(arrived, inverses):
    count = arrived.shape[0]
    lane = lax.broadcasted_iota(jnp.int32, (1, 4, SLOT, LANES), 3) // 32
    part = lax.broadcasted_iota(jnp.int32, (1, 4, SLOT, LANES), 1)
    spread_out = jnp.where(lane == part, arrived[:, None].astype(F32), 0.0)
    column = spread_out.reshape(count * 4 * SLOT, LANES).astype(BF)
    product = jnp.dot(inverses, column, preferred_element_type=F32)
    parts = []
    for s in range(inverses.shape[0] // 32):
        turned = product[32 * s : 32 * (s + 1)].T
        parts.append((turned[:32] + turned[32:64] + turned[64:96] + turned[96:]).astype(BF))
    return parts


def local_product(vector, inverse):
    rows = vector.shape[0]
    both = lax.dot_general(jnp.concatenate(split(vector), axis=0), inverse, NT, preferred_element_type=F32)
    return both[:rows] + both[rows:]


def image_blocks(extended, tiles, cols):
    blocks, width = tiles.shape[:2]
    rhs, order = extended.shape[1:]
    images = []
    for b in range(0, blocks, 2):
        pair = range(b, min(b + 2, blocks))
        vectors = [
            jnp.concatenate([extended[x]] + [extended[cols[x, t]] for t in range(width - 1)], axis=1) for x in pair
        ]
        rows = [jnp.concatenate([tiles[x, t] for t in range(width)], axis=1) for x in pair]
        both = lax.dot_general(
            jnp.concatenate(vectors, axis=0), jnp.concatenate(rows, axis=0), NT, preferred_element_type=F32
        )
        for k in range(len(pair)):
            images.append(both[rhs * k : rhs * (k + 1), order * k : order * (k + 1)])
    return images


def sums_row(upper, lower):
    return jnp.sum(jnp.concatenate([upper, lower, upper, lower], axis=0).T, axis=0, keepdims=True)


def chosen(sends, m, direction):
    return sum(jnp.where(direction == k, sends[m, k], 0) for k in range(sends.shape[1]))


def fetch(pairs, sems):
    copies = [pltpu.make_async_copy(source, target, sems.at[k]) for k, (source, target) in enumerate(pairs)]
    for copy in copies:
        copy.start()
    return copies


def start_kernel(
    send_hbm, right_hbm, block_inverse_hbm, basis_hbm, inverse_hbm,
    slot_hbm, right_ref, block_inverse_ref, basis_ref, inverse_ref, out0, out1, out2, out3,
    slot_ref, out_ref, send_ref, wide, sems, out_sems,
):
    copies = fetch(
        [
            (right_hbm, right_ref),
            (basis_hbm, basis_ref),
            (block_inverse_hbm, block_inverse_ref),
            (inverse_hbm, wide),
            (send_hbm, send_ref),
        ],
        sems,
    )
    blocks, rhs, order = right_ref.shape
    halo = send_ref.shape[0]
    total = wide.shape[1]
    for copy in copies[:2]:
        copy.wait()
    vectors = [right_ref[b] for b in range(blocks)]
    slot_ref[...] = jnp.broadcast_to(restrict_slot(vectors, basis_ref).astype(BF)[None], slot_ref.shape)
    leaving = fetch([(slot_ref, slot_hbm)], out_sems)
    copies[3].wait()
    inverse = wide[...].astype(BF)
    inverse_ref[...] = inverse
    copies[2].wait()
    copies[4].wait()
    for q, ((number, odd), out_hbm) in enumerate(zip(SWAPS, (out0, out1, out2, out3))):
        send, _, _ = swap_ends(number, odd)
        out_ref[q, :, :total] = inverse
        for m in range(halo):
            row = send_ref[m, send]
            out_ref[q, :, total + m * order : total + (m + 1) * order] = basis_ref[row]
            start = total + (halo + m) * order
            local = local_product(right_ref[row], block_inverse_ref[row])
            out_ref[q, :, start : start + order] = local.astype(BF)
        leaving += fetch([(out_ref.at[q], out_hbm)], out_sems.at[pl.ds(1 + q, 1)])
    for copy in leaving:
        copy.wait()


def gather_kernel(inverse_ref, basis_ref, right_ref, block_inverse_ref, tiles_hbm, cols_hbm, send_hbm, *refs):
    halos, refs = refs[: EARLY[0]], refs[EARLY[0] :]
    inverses_ref, bases_ref, locals_ref, tiles_ref, cols_ref, send_ref, local_ref, sems, tile_sems = refs
    rows, total = inverse_ref.shape
    blocks, _, order = basis_ref.shape
    copies = fetch([(cols_hbm, cols_ref), (send_hbm, send_ref)], sems)
    copies += fetch([(tiles_hbm.at[b], tiles_ref.at[b]) for b in range(tiles_ref.shape[0])], tile_sems)
    for b in range(blocks):
        local_ref[b] = local_product(right_ref[b], block_inverse_ref[b])
    inverses_ref[:rows] = inverse_ref[...]
    bases_ref[:blocks] = basis_ref[...]
    for q, ref in enumerate(halos):
        inverses_ref[rows * (1 + q) : rows * (2 + q)] = ref[:, :total]
        halo = (ref.shape[1] - total) // (2 * order)
        for m in range(halo):
            at = total + m * order
            bases_ref[blocks + halo * q + m] = ref[:, at : at + order]
            at += halo * order
            locals_ref[halo * q + m] = ref[:, at : at + order]
    for copy in copies:
        copy.wait()


def all_inverses(inverses_ref, late):
    total = inverses_ref.shape[1]
    return jnp.concatenate([inverses_ref[...]] + [ref[:, :total] for ref in late], axis=0)


def basis_block(k, bases_ref, late, total, halo):
    if k < bases_ref.shape[0]:
        return bases_ref[k]
    q, m = divmod(k - bases_ref.shape[0], halo)
    order = bases_ref.shape[2]
    return late[q][:, total + m * order : total + (m + 1) * order]


def pack(extended, k, value, blocks, halo):
    if k < blocks:
        extended[k] = value.astype(BF)
    else:
        q, m = divmod(k - blocks, halo)
        _, slot, valid = swap_ends(*SWAPS[q])
        extended[blocks + halo * slot + m] = jnp.where(valid, value, 0.0).astype(BF)


def owner(k, blocks, halo):
    return 0 if k < blocks else 1 + (k - blocks) // halo


def first_kernel(
    cols_ref, send_ref, arrived_ref, inverses_ref, bases_ref, local_ref, locals_ref, block_inverse_ref, right_ref,
    tiles_ref, *refs,
):
    late, refs = refs[: 4 - EARLY[0]], refs[4 - EARLY[0] :]
    slot_hbm, update_ref, image_ref, out0, out1, out2, out3 = refs[:7]
    slot_ref, out_ref, extended, out_sems = refs[7:]
    cols, sends = cols_ref[...], send_ref[...]
    blocks, rhs, order = right_ref.shape
    halo = sends.shape[0]
    total = inverses_ref.shape[1]
    coarse = coarse_parts(arrived_ref[...], all_inverses(inverses_ref, late))
    early = blocks + halo * EARLY[0]
    for k in range(update_ref.shape[0]):
        basis = basis_block(k, bases_ref, late, total, halo)
        if k < blocks:
            local = local_ref[k]
        elif k < early:
            local = locals_ref[k - blocks].astype(F32)
        else:
            q, m = divmod(k - early, halo)
            at = total + (halo + m) * order
            local = late[q][:, at : at + order].astype(F32)
        update = local + jnp.dot(coarse[owner(k, blocks, halo)], basis, preferred_element_type=F32)
        update_ref[k] = update
        pack(extended, k, update, blocks, halo)
    upper = lower = jnp.zeros((rhs, order), F32)
    images = image_blocks(extended, tiles_ref, cols)
    for b, image in enumerate(images):
        image_ref[b] = image
        upper += right_ref[b] * image
        lower += image * image
    row = sums_row(upper, lower)
    high, low = split(row)
    lane = lax.broadcasted_iota(jnp.int32, (1, LANES), 1)
    row = jnp.where(lane < 64, high.astype(F32), low.astype(F32))
    slot = restrict_slot(images, bases_ref)
    half = SLOT // 2
    whole = jnp.concatenate([slot[:half], slot[half:], jnp.broadcast_to(row, (half, LANES))], axis=1)
    slot_ref[...] = jnp.broadcast_to(whole.astype(BF)[None], slot_ref.shape)
    leaving = fetch([(slot_ref, slot_hbm)], out_sems)
    for q, ((number, odd), out_hbm) in enumerate(zip(SWAPS, (out0, out1, out2, out3))):
        send, _, _ = swap_ends(number, odd)
        for m in range(halo):
            row = chosen(sends, m, send)
            local = local_product(image_ref[row], block_inverse_ref[row])
            out_ref[q, :, m * order : (m + 1) * order] = local.astype(BF)
        leaving += fetch([(out_ref.at[q], out_hbm)], out_sems.at[pl.ds(1 + q, 1)])
    for copy in leaving:
        copy.wait()


def local_kernel(image_ref, block_inverse_ref, *refs):
    blocks, _, order = image_ref.shape
    local_ref = refs[-1]
    for b in range(blocks):
        local_ref[b] = local_product(image_ref[b], block_inverse_ref[b])
    for q, ref in enumerate(refs[:-1]):
        halo = ref.shape[1] // order
        for m in range(halo):
            local_ref[blocks + halo * q + m] = ref[:, m * order : (m + 1) * order].astype(F32)


def second_kernel(
    cols_ref, arrived_ref, inverses_ref, bases_ref, local_ref, update_ref, image_ref, right_ref, tiles_ref, *refs,
):
    late, refs = refs[: 4 - EARLY[0]], refs[4 - EARLY[0] :]
    nexts, refs = refs[: 4 - EARLY[1]], refs[4 - EARLY[1] :]
    slot_ref, scaled_ref, second_ref, residual_ref, image2_ref, extended = refs
    cols = cols_ref[...]
    blocks, rhs, order = right_ref.shape
    halo = (update_ref.shape[0] - blocks) // 4
    total = inverses_ref.shape[1]
    arrived = arrived_ref[...].astype(F32)
    restricted = jnp.concatenate([arrived[:, :, :LANES], arrived[:, :, LANES : 2 * LANES]], axis=1)
    coarse = coarse_parts(restricted, all_inverses(inverses_ref, late))
    sums = jnp.sum(arrived[:, :1, 2 * LANES :], axis=0)
    turned = jnp.broadcast_to(sums, (LANES, LANES)).T
    weight = (turned[:32] + turned[64:96]) / (turned[32:64] + turned[96:] + 1e-6)
    for k in range(update_ref.shape[0]):
        basis = basis_block(k, bases_ref, late, total, halo)
        if k < local_ref.shape[0]:
            local = local_ref[k]
        else:
            q, m = divmod(k - local_ref.shape[0], halo)
            local = nexts[q][:, m * order : (m + 1) * order].astype(F32)
        update = update_ref[k]
        spread = jnp.dot(coarse[owner(k, blocks, halo)], basis, preferred_element_type=F32)
        second = update - weight * (local + spread)
        if k < blocks:
            scaled_ref[k] = weight * update
            second_ref[k] = second
        pack(extended, k, second, blocks, halo)
    upper = lower = jnp.zeros((rhs, order), F32)
    for b, image in enumerate(image_blocks(extended, tiles_ref, cols)):
        residual = right_ref[b] - weight * image_ref[b]
        residual_ref[b] = residual
        image2_ref[b] = image
        upper += residual * image
        lower += image * image
    slot_ref[...] = jnp.broadcast_to(sums_row(upper, lower)[None], slot_ref.shape)


def last_kernel(arrived_ref, scaled_ref, second_ref, residual_ref, image_ref, solution_ref, out_ref):
    sums = jnp.sum(arrived_ref[...], axis=0)
    turned = jnp.broadcast_to(sums, (LANES, LANES)).T
    weight = turned[:32] / (turned[32:64] + 1e-6)
    for b in range(scaled_ref.shape[0]):
        solution_ref[b] = scaled_ref[b] + weight * second_ref[b]
        out_ref[b] = residual_ref[b] - weight * image_ref[b]


def call(kernel, inputs, places, outputs, scratch=(), flops=None):
    kinds = {"v": pltpu.VMEM, "h": pltpu.HBM}
    into, out = places.split(">")
    inputs = [pltpu.with_memory_space_constraint(x, pltpu.HBM) if p == "h" else x for x, p in zip(inputs, into)]
    return pl.pallas_call(
        kernel,
        out_shape=[
            pltpu.HBM(shape, dtype) if p == "h" else jax.ShapeDtypeStruct(shape, dtype)
            for (shape, dtype), p in zip(outputs, out)
        ],
        in_specs=[pl.BlockSpec(memory_space=kinds[p]) for p in into],
        out_specs=[pl.BlockSpec(memory_space=kinds[p]) for p in out],
        scratch_shapes=scratch,
        compiler_params=pltpu.CompilerParams(vmem_limit_bytes=32 * 1024 * 1024),
        cost_estimate=flops and pl.CostEstimate(flops=flops, bytes_accessed=0, transcendentals=0),
        name=kernel.__name__,
    )(*inputs)


def exchange(slots):
    return lax.all_to_all(slots, AXES, 0, 0, tiled=True)


def body(right_sides, tiles, tile_cols, send_rows, block_inverse, coarse_basis, coarse_inverse):
    blocks, rhs, order = right_sides.shape
    rows, total = coarse_inverse.shape
    halo = send_rows.shape[1]
    count = lax.axis_size("sx") * lax.axis_size("sy")
    field = (right_sides.shape, F32)
    sends = pltpu.SMEM((halo, send_rows.shape[0]), jnp.int32)
    turned_sends = send_rows.T
    extended = pltpu.VMEM((blocks + 4 * halo, rhs, order), BF)

    def sems(number):
        return pltpu.SemaphoreType.DMA((number,))

    def swapped(values):
        return [swap(value, number, odd) for value, (number, odd) in zip(values, SWAPS)]

    slots, right, inverses, basis, coarse_rows, *halos = call(
        start_kernel,
        (turned_sends, right_sides, block_inverse, coarse_basis, coarse_inverse),
        "hhhhh>hvvvvhhhh",
        [
            ((count, SLOT, LANES), BF),
            field,
            (block_inverse.shape, BF),
            (coarse_basis.shape, BF),
            (coarse_inverse.shape, BF),
        ]
        + [((rhs, total + 2 * halo * order), BF)] * 4,
        (
            pltpu.VMEM((count, SLOT, LANES), BF),
            pltpu.VMEM((4, rhs, total + 2 * halo * order), BF),
            sends,
            pltpu.VMEM(coarse_inverse.shape, F32),
            sems(5),
            sems(5),
        ),
    )
    halos = swapped(halos)
    early, late = halos[: EARLY[0]], halos[EARLY[0] :]
    arrived = exchange(slots)
    reach = blocks + halo * EARLY[0]
    coarse_rows, bases, locals_, blocks_of_a, tile_cols, turned_sends, local = call(
        gather_kernel,
        (coarse_rows, basis, right, inverses, tiles, tile_cols, turned_sends, *early),
        "vvvvhhh" + "v" * len(early) + ">vvvvvvv",
        [
            (((1 + EARLY[0]) * rows, total), BF),
            ((reach,) + coarse_basis.shape[1:], BF),
            ((max(reach - blocks, 1), rhs, order), BF),
            (tiles.shape, BF),
            (tile_cols.shape, jnp.int32),
            (turned_sends.shape, jnp.int32),
            field,
        ],
        (sems(2), sems(blocks)),
        flops=10**11 if EARLY[0] else None,
    )
    slots, update, image, *nexts = call(
        first_kernel,
        (tile_cols, turned_sends, arrived, coarse_rows, bases, local, locals_, inverses, right, blocks_of_a, *late),
        "vvvvvvvvvv" + "v" * len(late) + ">hvvhhhh",
        [((count, SLOT // 2, 3 * LANES), BF), ((blocks + 4 * halo, rhs, order), F32), field]
        + [((rhs, halo * order), BF)] * 4,
        (
            pltpu.VMEM((count, SLOT // 2, 3 * LANES), BF),
            pltpu.VMEM((4, rhs, halo * order), BF),
            extended,
            sems(5),
        ),
    )
    nexts = swapped(nexts)
    soon, nexts = nexts[: EARLY[1]], nexts[EARLY[1] :]
    arrived = exchange(slots)
    (local,) = call(
        local_kernel,
        (image, inverses, *soon),
        "vv" + "v" * len(soon) + ">v",
        [((blocks + halo * EARLY[1], rhs, order), F32)],
        flops=10**11 if EARLY[1] else None,
    )
    slots, scaled, second, residual, image = call(
        second_kernel,
        (tile_cols, arrived, coarse_rows, bases, local, update, image, right, blocks_of_a, *late, *nexts),
        "vvvvvvvvv" + "v" * (len(late) + len(nexts)) + ">vvvvv",
        [((count, 1, LANES), F32)] + [field] * 4,
        (extended,),
    )
    return tuple(call(last_kernel, (exchange(slots), scaled, second, residual, image), "vvvvv>vv", [field] * 2))


def solution(mesh):
    block3 = P(AXES, None, None)
    placed = (block3, P(AXES, None, None, None), P(AXES, None), P(AXES, None), block3, block3, P(AXES, None))
    return jax.shard_map(body, mesh=mesh, in_specs=placed, out_specs=(block3, block3), check_vma=False)
```

```python
import functools

import jax
import jax.numpy as jnp
from jax import lax
from jax.experimental import pallas as pl
from jax.experimental.pallas import tpu as pltpu
from jax.sharding import PartitionSpec as P

AXES = ("sx", "sy")
BF = jnp.bfloat16
F32 = jnp.float32
NT = (((1,), (1,)), ((), ()))
LANES = 128
SLOT = 8
SWAPS = ((1, True), (0, True), (1, False), (0, False))
EARLY = 1, 0


def swap(value, number, odd):
    counts = [lax.axis_size(axis) for axis in AXES]
    pairs = []
    for device in range(counts[0] * counts[1]):
        place = list(divmod(device, counts[1]))
        other = place[number] + (1 if (place[number] % 2 == 0) != odd else -1)
        if 0 <= other < counts[number]:
            place[number] = other
        else:
            place[1 - number] ^= 2 if number == 0 and counts[1] % 4 == 0 else 1
        pairs.append((device, place[0] * counts[1] + place[1]))
    return lax.ppermute(value, AXES, pairs)


def swap_ends(number, odd):
    axis = AXES[number]
    place, count = lax.axis_index(axis), lax.axis_size(axis)
    up = (lax.rem(place, 2) == 0) != odd
    send = 2 * number + jnp.where(up, 0, 1)
    slot = 2 * number + jnp.where(up, 1, 0)
    valid = jnp.where(up, place < count - 1, place > 0)
    return send, slot, valid


def split(value):
    high = value.astype(BF)
    return high, (value - high.astype(F32)).astype(BF)


def restrict_slot(vectors, basis_ref):
    left, right = [], []
    for b, vector in enumerate(vectors):
        for part in split(vector):
            left.append(basis_ref[b])
            right.append(jnp.concatenate([part] * 4, axis=0))
    full = lax.dot_general(
        jnp.concatenate(left, axis=1), jnp.concatenate(right, axis=1), NT, preferred_element_type=F32
    )
    group = lax.broadcasted_iota(jnp.int32, (SLOT, LANES), 1) // 32
    slot = full[:SLOT]
    for j in range(1, 4):
        slot = jnp.where(group == j, full[SLOT * j : SLOT * (j + 1)], slot)
    return slot


def coarse_parts(arrived, inverses):
    count = arrived.shape[0]
    lane = lax.broadcasted_iota(jnp.int32, (1, 4, SLOT, LANES), 3) // 32
    part = lax.broadcasted_iota(jnp.int32, (1, 4, SLOT, LANES), 1)
    spread_out = jnp.where(lane == part, arrived[:, None], 0.0)
    column = spread_out.reshape(count * 4 * SLOT, LANES).astype(BF)
    product = jnp.dot(inverses, column, preferred_element_type=F32)
    parts = []
    for s in range(inverses.shape[0] // 32):
        turned = product[32 * s : 32 * (s + 1)].T
        parts.append((turned[:32] + turned[32:64] + turned[64:96] + turned[96:]).astype(BF))
    return parts


def local_product(vector, inverse):
    rows = vector.shape[0]
    both = lax.dot_general(jnp.concatenate(split(vector), axis=0), inverse, NT, preferred_element_type=F32)
    return both[:rows] + both[rows:]


def image_blocks(extended, tiles, cols):
    blocks, width = tiles.shape[:2]
    rhs, order = extended.shape[1:]
    images = []
    for b in range(0, blocks, 2):
        pair = range(b, min(b + 2, blocks))
        vectors = [
            jnp.concatenate([extended[x]] + [extended[cols[x, t]] for t in range(width - 1)], axis=1) for x in pair
        ]
        rows = [jnp.concatenate([tiles[x, t] for t in range(width)], axis=1) for x in pair]
        both = lax.dot_general(
            jnp.concatenate(vectors, axis=0), jnp.concatenate(rows, axis=0), NT, preferred_element_type=F32
        )
        for k in range(len(pair)):
            images.append(both[rhs * k : rhs * (k + 1), order * k : order * (k + 1)])
    return images


def sums_row(upper, lower):
    return jnp.sum(jnp.concatenate([upper, lower, upper, lower], axis=0).T, axis=0, keepdims=True)


def repeated(slot, shape):
    return jnp.broadcast_to(slot[None], (shape[0] // slot.shape[0],) + slot.shape).reshape(shape).astype(BF)


def chosen(sends, m, direction):
    return sum(jnp.where(direction == k, sends[m, k], 0) for k in range(sends.shape[1]))


def fetch(pairs, sems):
    copies = [pltpu.make_async_copy(source, target, sems.at[k]) for k, (source, target) in enumerate(pairs)]
    for copy in copies:
        copy.start()
    return copies


def start_kernel(
    send_hbm, right_hbm, block_inverse_hbm, basis_hbm, inverse_hbm,
    slot_hbm, right_ref, block_inverse_ref, basis_ref, inverse_ref, out0, out1, out2, out3,
    slot_ref, out_ref, send_ref, wide, sems, out_sems,
):
    copies = fetch(
        [
            (right_hbm, right_ref),
            (basis_hbm, basis_ref),
            (block_inverse_hbm, block_inverse_ref),
            (inverse_hbm, wide),
            (send_hbm, send_ref),
        ],
        sems,
    )
    blocks, rhs, order = right_ref.shape
    halo = send_ref.shape[0]
    total = wide.shape[1]
    for copy in copies[:2]:
        copy.wait()
    vectors = [right_ref[b] for b in range(blocks)]
    slot_ref[...] = repeated(restrict_slot(vectors, basis_ref), slot_ref.shape)
    leaving = fetch([(slot_ref, slot_hbm)], out_sems)
    copies[3].wait()
    inverse = wide[...].astype(BF)
    inverse_ref[...] = inverse
    copies[2].wait()
    copies[4].wait()
    for q, ((number, odd), out_hbm) in enumerate(zip(SWAPS, (out0, out1, out2, out3))):
        send, _, _ = swap_ends(number, odd)
        out_ref[q, :, :total] = inverse
        for m in range(halo):
            row = send_ref[m, send]
            out_ref[q, :, total + m * order : total + (m + 1) * order] = basis_ref[row]
            start = total + (halo + m) * order
            local = local_product(right_ref[row], block_inverse_ref[row])
            out_ref[q, :, start : start + order] = local.astype(BF)
        leaving += fetch([(out_ref.at[q], out_hbm)], out_sems.at[pl.ds(1 + q, 1)])
    for copy in leaving:
        copy.wait()


def gather_kernel(inverse_ref, basis_ref, right_ref, block_inverse_ref, tiles_hbm, cols_hbm, send_hbm, *refs):
    halos, refs = refs[: EARLY[0]], refs[EARLY[0] :]
    inverses_ref, bases_ref, locals_ref, tiles_ref, cols_ref, send_ref, local_ref, sems, tile_sems = refs
    rows, total = inverse_ref.shape
    blocks, _, order = basis_ref.shape
    copies = fetch([(cols_hbm, cols_ref), (send_hbm, send_ref)], sems)
    copies += fetch([(tiles_hbm.at[b], tiles_ref.at[b]) for b in range(tiles_ref.shape[0])], tile_sems)
    for b in range(blocks):
        local_ref[b] = local_product(right_ref[b], block_inverse_ref[b])
    inverses_ref[:rows] = inverse_ref[...]
    bases_ref[:blocks] = basis_ref[...]
    for q, ref in enumerate(halos):
        inverses_ref[rows * (1 + q) : rows * (2 + q)] = ref[:, :total]
        halo = (ref.shape[1] - total) // (2 * order)
        for m in range(halo):
            at = total + m * order
            bases_ref[blocks + halo * q + m] = ref[:, at : at + order]
            at += halo * order
            locals_ref[halo * q + m] = ref[:, at : at + order]
    for copy in copies:
        copy.wait()


def all_inverses(inverses_ref, late):
    total = inverses_ref.shape[1]
    return jnp.concatenate([inverses_ref[...]] + [ref[:, :total] for ref in late], axis=0)


def basis_block(k, bases_ref, late, total, halo):
    if k < bases_ref.shape[0]:
        return bases_ref[k]
    q, m = divmod(k - bases_ref.shape[0], halo)
    order = bases_ref.shape[2]
    return late[q][:, total + m * order : total + (m + 1) * order]


def pack(extended, k, value, blocks, halo):
    if k < blocks:
        extended[k] = value.astype(BF)
    else:
        q, m = divmod(k - blocks, halo)
        _, slot, valid = swap_ends(*SWAPS[q])
        extended[blocks + halo * slot + m] = jnp.where(valid, value, 0.0).astype(BF)


def owner(k, blocks, halo):
    return 0 if k < blocks else 1 + (k - blocks) // halo


def first_kernel(
    cols_ref, send_ref, arrived_ref, inverses_ref, bases_ref, local_ref, locals_ref, block_inverse_ref, right_ref,
    tiles_ref, *refs,
):
    late, refs = refs[: 4 - EARLY[0]], refs[4 - EARLY[0] :]
    slot_hbm, update_ref, image_ref, out0, out1, out2, out3 = refs[:7]
    slot_ref, out_ref, extended, out_sems = refs[7:]
    cols, sends = cols_ref[...], send_ref[...]
    blocks, rhs, order = right_ref.shape
    halo = sends.shape[0]
    total = inverses_ref.shape[1]
    arrived = arrived_ref[...].astype(F32).reshape(-1, SLOT, LANES)
    coarse = coarse_parts(arrived, all_inverses(inverses_ref, late))
    early = blocks + halo * EARLY[0]
    for k in range(update_ref.shape[0]):
        basis = basis_block(k, bases_ref, late, total, halo)
        if k < blocks:
            local = local_ref[k]
        elif k < early:
            local = locals_ref[k - blocks].astype(F32)
        else:
            q, m = divmod(k - early, halo)
            at = total + (halo + m) * order
            local = late[q][:, at : at + order].astype(F32)
        update = local + jnp.dot(coarse[owner(k, blocks, halo)], basis, preferred_element_type=F32)
        update_ref[k] = update
        pack(extended, k, update, blocks, halo)
    upper = lower = jnp.zeros((rhs, order), F32)
    images = image_blocks(extended, tiles_ref, cols)
    for b, image in enumerate(images):
        image_ref[b] = image
        upper += right_ref[b] * image
        lower += image * image
    row = sums_row(upper, lower)
    high, low = split(row)
    lane = lax.broadcasted_iota(jnp.int32, (1, LANES), 1)
    row = jnp.where(lane < 64, high.astype(F32), low.astype(F32))
    whole = jnp.concatenate([restrict_slot(images, bases_ref), jnp.broadcast_to(row, (SLOT, LANES))], axis=0)
    slot_ref[...] = repeated(whole, slot_ref.shape)
    leaving = fetch([(slot_ref, slot_hbm)], out_sems)
    for q, ((number, odd), out_hbm) in enumerate(zip(SWAPS, (out0, out1, out2, out3))):
        send, _, _ = swap_ends(number, odd)
        for m in range(halo):
            row = chosen(sends, m, send)
            local = local_product(image_ref[row], block_inverse_ref[row])
            out_ref[q, :, m * order : (m + 1) * order] = local.astype(BF)
        leaving += fetch([(out_ref.at[q], out_hbm)], out_sems.at[pl.ds(1 + q, 1)])
    for copy in leaving:
        copy.wait()


def local_kernel(image_ref, block_inverse_ref, *refs):
    blocks, _, order = image_ref.shape
    local_ref = refs[-1]
    for b in range(blocks):
        local_ref[b] = local_product(image_ref[b], block_inverse_ref[b])
    for q, ref in enumerate(refs[:-1]):
        halo = ref.shape[1] // order
        for m in range(halo):
            local_ref[blocks + halo * q + m] = ref[:, m * order : (m + 1) * order].astype(F32)


def second_kernel(
    cols_ref, arrived_ref, inverses_ref, bases_ref, local_ref, update_ref, image_ref, right_ref, tiles_ref, *refs,
):
    late, refs = refs[: 4 - EARLY[0]], refs[4 - EARLY[0] :]
    nexts, refs = refs[: 4 - EARLY[1]], refs[4 - EARLY[1] :]
    slot_ref, scaled_ref, second_ref, residual_ref, image2_ref, extended = refs
    cols = cols_ref[...]
    blocks, rhs, order = right_ref.shape
    halo = (update_ref.shape[0] - blocks) // 4
    total = inverses_ref.shape[1]
    arrived = arrived_ref[...].astype(F32).reshape(-1, 2 * SLOT, LANES)
    coarse = coarse_parts(arrived[:, :SLOT], all_inverses(inverses_ref, late))
    sums = jnp.sum(arrived[:, SLOT : SLOT + 1], axis=0)
    turned = jnp.broadcast_to(sums, (LANES, LANES)).T
    weight = (turned[:32] + turned[64:96]) / (turned[32:64] + turned[96:] + 1e-6)
    for k in range(update_ref.shape[0]):
        basis = basis_block(k, bases_ref, late, total, halo)
        if k < local_ref.shape[0]:
            local = local_ref[k]
        else:
            q, m = divmod(k - local_ref.shape[0], halo)
            local = nexts[q][:, m * order : (m + 1) * order].astype(F32)
        update = update_ref[k]
        spread = jnp.dot(coarse[owner(k, blocks, halo)], basis, preferred_element_type=F32)
        second = update - weight * (local + spread)
        if k < blocks:
            scaled_ref[k] = weight * update
            second_ref[k] = second
        pack(extended, k, second, blocks, halo)
    upper = lower = jnp.zeros((rhs, order), F32)
    for b, image in enumerate(image_blocks(extended, tiles_ref, cols)):
        residual = right_ref[b] - weight * image_ref[b]
        residual_ref[b] = residual
        image2_ref[b] = image
        upper += residual * image
        lower += image * image
    slot_ref[...] = jnp.broadcast_to(sums_row(upper, lower)[None], slot_ref.shape)


def last_kernel(arrived_ref, scaled_ref, second_ref, residual_ref, image_ref, solution_ref, out_ref):
    sums = jnp.sum(arrived_ref[...], axis=0)
    turned = jnp.broadcast_to(sums, (LANES, LANES)).T
    weight = turned[:32] / (turned[32:64] + 1e-6)
    for b in range(scaled_ref.shape[0]):
        solution_ref[b] = scaled_ref[b] + weight * second_ref[b]
        out_ref[b] = residual_ref[b] - weight * image_ref[b]


def call(kernel, inputs, places, outputs, scratch=(), flops=None):
    kinds = {"v": pltpu.VMEM, "h": pltpu.HBM}
    into, out = places.split(">")
    inputs = [pltpu.with_memory_space_constraint(x, pltpu.HBM) if p == "h" else x for x, p in zip(inputs, into)]
    return pl.pallas_call(
        kernel,
        out_shape=[
            pltpu.HBM(shape, dtype) if p == "h" else jax.ShapeDtypeStruct(shape, dtype)
            for (shape, dtype), p in zip(outputs, out)
        ],
        in_specs=[pl.BlockSpec(memory_space=kinds[p]) for p in into],
        out_specs=[pl.BlockSpec(memory_space=kinds[p]) for p in out],
        scratch_shapes=scratch,
        compiler_params=pltpu.CompilerParams(vmem_limit_bytes=32 * 1024 * 1024),
        cost_estimate=flops and pl.CostEstimate(flops=flops, bytes_accessed=0, transcendentals=0),
        name=kernel.__name__,
    )(*inputs)


def exchange(slots):
    count = lax.axis_size("sx") * lax.axis_size("sy")
    split_up = slots.reshape(count, -1, slots.shape[-1])
    return lax.all_to_all(split_up, AXES, 0, 0, tiled=True).reshape(slots.shape)


def body(right_sides, tiles, tile_cols, send_rows, block_inverse, coarse_basis, coarse_inverse):
    blocks, rhs, order = right_sides.shape
    rows, total = coarse_inverse.shape
    halo = send_rows.shape[1]
    count = lax.axis_size("sx") * lax.axis_size("sy")
    field = (right_sides.shape, F32)
    sends = pltpu.SMEM((halo, send_rows.shape[0]), jnp.int32)
    turned_sends = send_rows.T
    extended = pltpu.VMEM((blocks + 4 * halo, rhs, order), BF)

    def sems(number):
        return pltpu.SemaphoreType.DMA((number,))

    def swapped(values):
        return [swap(value, number, odd) for value, (number, odd) in zip(values, SWAPS)]

    slots, right, inverses, basis, coarse_rows, *halos = call(
        start_kernel,
        (turned_sends, right_sides, block_inverse, coarse_basis, coarse_inverse),
        "hhhhh>hvvvvhhhh",
        [
            ((count * SLOT, LANES), BF),
            field,
            (block_inverse.shape, BF),
            (coarse_basis.shape, BF),
            (coarse_inverse.shape, BF),
        ]
        + [((rhs, total + 2 * halo * order), BF)] * 4,
        (
            pltpu.VMEM((count * SLOT, LANES), BF),
            pltpu.VMEM((4, rhs, total + 2 * halo * order), BF),
            sends,
            pltpu.VMEM(coarse_inverse.shape, F32),
            sems(5),
            sems(5),
        ),
    )
    halos = swapped(halos)
    early, late = halos[: EARLY[0]], halos[EARLY[0] :]
    arrived = exchange(slots)
    reach = blocks + halo * EARLY[0]
    coarse_rows, bases, locals_, blocks_of_a, tile_cols, turned_sends, local = call(
        gather_kernel,
        (coarse_rows, basis, right, inverses, tiles, tile_cols, turned_sends, *early),
        "vvvvhhh" + "v" * len(early) + ">vvvvvvv",
        [
            (((1 + EARLY[0]) * rows, total), BF),
            ((reach,) + coarse_basis.shape[1:], BF),
            ((max(reach - blocks, 1), rhs, order), BF),
            (tiles.shape, BF),
            (tile_cols.shape, jnp.int32),
            (turned_sends.shape, jnp.int32),
            field,
        ],
        (sems(2), sems(blocks)),
        flops=10**11 if EARLY[0] else None,
    )
    slots, update, image, *nexts = call(
        first_kernel,
        (tile_cols, turned_sends, arrived, coarse_rows, bases, local, locals_, inverses, right, blocks_of_a, *late),
        "vvvvvvvvvv" + "v" * len(late) + ">hvvhhhh",
        [((count * 2 * SLOT, LANES), BF), ((blocks + 4 * halo, rhs, order), F32), field]
        + [((rhs, halo * order), BF)] * 4,
        (
            pltpu.VMEM((count * 2 * SLOT, LANES), BF),
            pltpu.VMEM((4, rhs, halo * order), BF),
            extended,
            sems(5),
        ),
    )
    nexts = swapped(nexts)
    soon, nexts = nexts[: EARLY[1]], nexts[EARLY[1] :]
    arrived = exchange(slots)
    (local,) = call(
        local_kernel,
        (image, inverses, *soon),
        "vv" + "v" * len(soon) + ">v",
        [((blocks + halo * EARLY[1], rhs, order), F32)],
        flops=10**11 if EARLY[1] else None,
    )
    slots, scaled, second, residual, image = call(
        second_kernel,
        (tile_cols, arrived, coarse_rows, bases, local, update, image, right, blocks_of_a, *late, *nexts),
        "vvvvvvvvv" + "v" * (len(late) + len(nexts)) + ">vvvvv",
        [((count, 1, LANES), F32)] + [field] * 4,
        (extended,),
    )
    return tuple(call(last_kernel, (exchange(slots), scaled, second, residual, image), "vvvvv>vv", [field] * 2))


def solution(mesh):
    block3 = P(AXES, None, None)
    placed = (block3, P(AXES, None, None, None), P(AXES, None), P(AXES, None), block3, block3, P(AXES, None))
    return jax.shard_map(body, mesh=mesh, in_specs=placed, out_specs=(block3, block3), check_vma=False)
```

```python
import functools

import jax
import jax.numpy as jnp
from jax import lax
from jax.experimental import pallas as pl
from jax.experimental.pallas import tpu as pltpu
from jax.sharding import PartitionSpec as P

AXES = ("sx", "sy")
BF = jnp.bfloat16
F32 = jnp.float32
NT = (((1,), (1,)), ((), ()))
LANES = 128
SLOT = 8
SWAPS = ((1, True), (0, True), (1, False), (0, False))
EARLY = 1, 0


def swap(value, number, odd):
    counts = [lax.axis_size(axis) for axis in AXES]
    pairs = []
    for device in range(counts[0] * counts[1]):
        place = list(divmod(device, counts[1]))
        other = place[number] + (1 if (place[number] % 2 == 0) != odd else -1)
        if 0 <= other < counts[number]:
            place[number] = other
        else:
            place[1 - number] ^= 2 if number == 0 and counts[1] % 4 == 0 else 1
        pairs.append((device, place[0] * counts[1] + place[1]))
    return lax.ppermute(value, AXES, pairs)


def swap_ends(number, odd):
    axis = AXES[number]
    place, count = lax.axis_index(axis), lax.axis_size(axis)
    up = (lax.rem(place, 2) == 0) != odd
    send = 2 * number + jnp.where(up, 0, 1)
    slot = 2 * number + jnp.where(up, 1, 0)
    valid = jnp.where(up, place < count - 1, place > 0)
    return send, slot, valid


def split(value):
    high = value.astype(BF)
    return high, (value - high.astype(F32)).astype(BF)


def restrict_slot(vectors, basis_ref, parts=2):
    left, right = [], []
    for b, vector in enumerate(vectors):
        for part in split(vector)[:parts]:
            left.append(basis_ref[b])
            right.append(jnp.concatenate([part] * 4, axis=0))
    full = lax.dot_general(
        jnp.concatenate(left, axis=1), jnp.concatenate(right, axis=1), NT, preferred_element_type=F32
    )
    group = lax.broadcasted_iota(jnp.int32, (SLOT, LANES), 1) // 32
    slot = full[:SLOT]
    for j in range(1, 4):
        slot = jnp.where(group == j, full[SLOT * j : SLOT * (j + 1)], slot)
    return slot


def coarse_parts(arrived, inverses):
    count = arrived.shape[0]
    lane = lax.broadcasted_iota(jnp.int32, (1, 4, SLOT, LANES), 3) // 32
    part = lax.broadcasted_iota(jnp.int32, (1, 4, SLOT, LANES), 1)
    spread_out = jnp.where(lane == part, arrived[:, None], 0.0)
    column = spread_out.reshape(count * 4 * SLOT, LANES).astype(BF)
    product = jnp.dot(inverses, column, preferred_element_type=F32)
    parts = []
    for s in range(inverses.shape[0] // 32):
        turned = product[32 * s : 32 * (s + 1)].T
        parts.append((turned[:32] + turned[32:64] + turned[64:96] + turned[96:]).astype(BF))
    return parts


def local_product(vector, inverse):
    rows = vector.shape[0]
    both = lax.dot_general(jnp.concatenate(split(vector), axis=0), inverse, NT, preferred_element_type=F32)
    return both[:rows] + both[rows:]


def image_blocks(extended, tiles, cols):
    blocks, width = tiles.shape[:2]
    rhs, order = extended.shape[1:]
    images = []
    for b in range(0, blocks, 2):
        pair = range(b, min(b + 2, blocks))
        vectors = [
            jnp.concatenate([extended[x]] + [extended[cols[x, t]] for t in range(width - 1)], axis=1) for x in pair
        ]
        rows = [jnp.concatenate([tiles[x, t] for t in range(width)], axis=1) for x in pair]
        both = lax.dot_general(
            jnp.concatenate(vectors, axis=0), jnp.concatenate(rows, axis=0), NT, preferred_element_type=F32
        )
        for k in range(len(pair)):
            images.append(both[rhs * k : rhs * (k + 1), order * k : order * (k + 1)])
    return images


def sums_row(upper, lower):
    return jnp.sum(jnp.concatenate([upper, lower, upper, lower], axis=0).T, axis=0, keepdims=True)


def repeated(slot, shape):
    return jnp.broadcast_to(slot[None], (shape[0] // slot.shape[0],) + slot.shape).reshape(shape).astype(BF)


def chosen(sends, m, direction):
    return sum(jnp.where(direction == k, sends[m, k], 0) for k in range(sends.shape[1]))


def fetch(pairs, sems):
    copies = [pltpu.make_async_copy(source, target, sems.at[k]) for k, (source, target) in enumerate(pairs)]
    for copy in copies:
        copy.start()
    return copies


def start_kernel(
    send_hbm, right_hbm, block_inverse_hbm, basis_hbm, inverse_hbm,
    slot_hbm, right_ref, block_inverse_ref, basis_ref, inverse_ref, out0, out1, out2, out3,
    slot_ref, out_ref, send_ref, wide, sems, out_sems,
):
    copies = fetch(
        [
            (right_hbm, right_ref),
            (basis_hbm, basis_ref),
            (block_inverse_hbm, block_inverse_ref),
            (inverse_hbm, wide),
            (send_hbm, send_ref),
        ],
        sems,
    )
    blocks, rhs, order = right_ref.shape
    halo = send_ref.shape[0]
    total = wide.shape[1]
    for copy in copies[:2]:
        copy.wait()
    vectors = [right_ref[b] for b in range(blocks)]
    slot_ref[...] = repeated(restrict_slot(vectors, basis_ref, 1), slot_ref.shape)
    leaving = fetch([(slot_ref, slot_hbm)], out_sems)
    copies[3].wait()
    inverse = wide[...].astype(BF)
    inverse_ref[...] = inverse
    copies[2].wait()
    copies[4].wait()
    for q, ((number, odd), out_hbm) in enumerate(zip(SWAPS, (out0, out1, out2, out3))):
        send, _, _ = swap_ends(number, odd)
        out_ref[q, :, :total] = inverse
        for m in range(halo):
            row = send_ref[m, send]
            out_ref[q, :, total + m * order : total + (m + 1) * order] = basis_ref[row]
            start = total + (halo + m) * order
            local = local_product(right_ref[row], block_inverse_ref[row])
            out_ref[q, :, start : start + order] = local.astype(BF)
        leaving += fetch([(out_ref.at[q], out_hbm)], out_sems.at[pl.ds(1 + q, 1)])
    for copy in leaving:
        copy.wait()


def gather_kernel(inverse_ref, basis_ref, right_ref, block_inverse_ref, tiles_hbm, cols_hbm, send_hbm, *refs):
    halos, refs = refs[: EARLY[0]], refs[EARLY[0] :]
    inverses_ref, bases_ref, locals_ref, tiles_ref, cols_ref, send_ref, local_ref, sems, tile_sems = refs
    rows, total = inverse_ref.shape
    blocks, _, order = basis_ref.shape
    copies = fetch([(cols_hbm, cols_ref), (send_hbm, send_ref)], sems)
    copies += fetch([(tiles_hbm.at[b], tiles_ref.at[b]) for b in range(tiles_ref.shape[0])], tile_sems)
    for b in range(blocks):
        local_ref[b] = local_product(right_ref[b], block_inverse_ref[b])
    inverses_ref[:rows] = inverse_ref[...]
    bases_ref[:blocks] = basis_ref[...]
    for q, ref in enumerate(halos):
        inverses_ref[rows * (1 + q) : rows * (2 + q)] = ref[:, :total]
        halo = (ref.shape[1] - total) // (2 * order)
        for m in range(halo):
            at = total + m * order
            bases_ref[blocks + halo * q + m] = ref[:, at : at + order]
            at += halo * order
            locals_ref[halo * q + m] = ref[:, at : at + order]
    for copy in copies:
        copy.wait()


def all_inverses(inverses_ref, late):
    total = inverses_ref.shape[1]
    return jnp.concatenate([inverses_ref[...]] + [ref[:, :total] for ref in late], axis=0)


def basis_block(k, bases_ref, late, total, halo):
    if k < bases_ref.shape[0]:
        return bases_ref[k]
    q, m = divmod(k - bases_ref.shape[0], halo)
    order = bases_ref.shape[2]
    return late[q][:, total + m * order : total + (m + 1) * order]


def pack(extended, k, value, blocks, halo):
    if k < blocks:
        extended[k] = value.astype(BF)
    else:
        q, m = divmod(k - blocks, halo)
        _, slot, valid = swap_ends(*SWAPS[q])
        extended[blocks + halo * slot + m] = jnp.where(valid, value, 0.0).astype(BF)


def owner(k, blocks, halo):
    return 0 if k < blocks else 1 + (k - blocks) // halo


def first_kernel(
    cols_ref, send_ref, arrived_ref, inverses_ref, bases_ref, local_ref, locals_ref, block_inverse_ref, right_ref,
    tiles_ref, *refs,
):
    late, refs = refs[: 4 - EARLY[0]], refs[4 - EARLY[0] :]
    slot_hbm, update_ref, image_ref, out0, out1, out2, out3 = refs[:7]
    slot_ref, out_ref, extended, out_sems = refs[7:]
    cols, sends = cols_ref[...], send_ref[...]
    blocks, rhs, order = right_ref.shape
    halo = sends.shape[0]
    total = inverses_ref.shape[1]
    arrived = arrived_ref[...].astype(F32).reshape(-1, SLOT, LANES)
    coarse = coarse_parts(arrived, all_inverses(inverses_ref, late))
    early = blocks + halo * EARLY[0]
    for k in range(update_ref.shape[0]):
        basis = basis_block(k, bases_ref, late, total, halo)
        if k < blocks:
            local = local_ref[k]
        elif k < early:
            local = locals_ref[k - blocks].astype(F32)
        else:
            q, m = divmod(k - early, halo)
            at = total + (halo + m) * order
            local = late[q][:, at : at + order].astype(F32)
        update = local + jnp.dot(coarse[owner(k, blocks, halo)], basis, preferred_element_type=F32)
        update_ref[k] = update
        pack(extended, k, update, blocks, halo)
    upper = lower = jnp.zeros((rhs, order), F32)
    images = image_blocks(extended, tiles_ref, cols)
    for b, image in enumerate(images):
        image_ref[b] = image
        upper += right_ref[b] * image
        lower += image * image
    row = sums_row(upper, lower)
    high, low = split(row)
    lane = lax.broadcasted_iota(jnp.int32, (1, LANES), 1)
    row = jnp.where(lane < 64, high.astype(F32), low.astype(F32))
    whole = jnp.concatenate([restrict_slot(images, bases_ref), jnp.broadcast_to(row, (SLOT, LANES))], axis=0)
    slot_ref[...] = repeated(whole, slot_ref.shape)
    leaving = fetch([(slot_ref, slot_hbm)], out_sems)
    for q, ((number, odd), out_hbm) in enumerate(zip(SWAPS, (out0, out1, out2, out3))):
        send, _, _ = swap_ends(number, odd)
        for m in range(halo):
            row = chosen(sends, m, send)
            local = local_product(image_ref[row], block_inverse_ref[row])
            out_ref[q, :, m * order : (m + 1) * order] = local.astype(BF)
        leaving += fetch([(out_ref.at[q], out_hbm)], out_sems.at[pl.ds(1 + q, 1)])
    for copy in leaving:
        copy.wait()


def local_kernel(image_ref, block_inverse_ref, *refs):
    blocks, _, order = image_ref.shape
    local_ref = refs[-1]
    for b in range(blocks):
        local_ref[b] = local_product(image_ref[b], block_inverse_ref[b])
    for q, ref in enumerate(refs[:-1]):
        halo = ref.shape[1] // order
        for m in range(halo):
            local_ref[blocks + halo * q + m] = ref[:, m * order : (m + 1) * order].astype(F32)


def second_kernel(
    cols_ref, arrived_ref, inverses_ref, bases_ref, local_ref, update_ref, image_ref, right_ref, tiles_ref, *refs,
):
    late, refs = refs[: 4 - EARLY[0]], refs[4 - EARLY[0] :]
    nexts, refs = refs[: 4 - EARLY[1]], refs[4 - EARLY[1] :]
    slot_ref, scaled_ref, second_ref, residual_ref, image2_ref, extended = refs
    cols = cols_ref[...]
    blocks, rhs, order = right_ref.shape
    halo = (update_ref.shape[0] - blocks) // 4
    total = inverses_ref.shape[1]
    arrived = arrived_ref[...].astype(F32).reshape(-1, 2 * SLOT, LANES)
    coarse = coarse_parts(arrived[:, :SLOT], all_inverses(inverses_ref, late))
    sums = jnp.sum(arrived[:, SLOT : SLOT + 1], axis=0)
    turned = jnp.broadcast_to(sums, (LANES, LANES)).T
    weight = (turned[:32] + turned[64:96]) / (turned[32:64] + turned[96:] + 1e-6)
    for k in range(update_ref.shape[0]):
        basis = basis_block(k, bases_ref, late, total, halo)
        if k < local_ref.shape[0]:
            local = local_ref[k]
        else:
            q, m = divmod(k - local_ref.shape[0], halo)
            local = nexts[q][:, m * order : (m + 1) * order].astype(F32)
        update = update_ref[k]
        spread = jnp.dot(coarse[owner(k, blocks, halo)], basis, preferred_element_type=F32)
        second = update - weight * (local + spread)
        if k < blocks:
            scaled_ref[k] = weight * update
            second_ref[k] = second
        pack(extended, k, second, blocks, halo)
    upper = lower = jnp.zeros((rhs, order), F32)
    for b, image in enumerate(image_blocks(extended, tiles_ref, cols)):
        residual = right_ref[b] - weight * image_ref[b]
        residual_ref[b] = residual
        image2_ref[b] = image
        upper += residual * image
        lower += image * image
    slot_ref[...] = jnp.broadcast_to(sums_row(upper, lower)[None], slot_ref.shape)


def last_kernel(arrived_ref, scaled_ref, second_ref, residual_ref, image_ref, solution_ref, out_ref):
    sums = jnp.sum(arrived_ref[...], axis=0)
    turned = jnp.broadcast_to(sums, (LANES, LANES)).T
    weight = turned[:32] / (turned[32:64] + 1e-6)
    for b in range(scaled_ref.shape[0]):
        solution_ref[b] = scaled_ref[b] + weight * second_ref[b]
        out_ref[b] = residual_ref[b] - weight * image_ref[b]


def call(kernel, inputs, places, outputs, scratch=(), flops=None):
    kinds = {"v": pltpu.VMEM, "h": pltpu.HBM}
    into, out = places.split(">")
    inputs = [pltpu.with_memory_space_constraint(x, pltpu.HBM) if p == "h" else x for x, p in zip(inputs, into)]
    return pl.pallas_call(
        kernel,
        out_shape=[
            pltpu.HBM(shape, dtype) if p == "h" else jax.ShapeDtypeStruct(shape, dtype)
            for (shape, dtype), p in zip(outputs, out)
        ],
        in_specs=[pl.BlockSpec(memory_space=kinds[p]) for p in into],
        out_specs=[pl.BlockSpec(memory_space=kinds[p]) for p in out],
        scratch_shapes=scratch,
        compiler_params=pltpu.CompilerParams(vmem_limit_bytes=32 * 1024 * 1024),
        cost_estimate=flops and pl.CostEstimate(flops=flops, bytes_accessed=0, transcendentals=0),
        name=kernel.__name__,
    )(*inputs)


def exchange(slots):
    count = lax.axis_size("sx") * lax.axis_size("sy")
    split_up = slots.reshape(count, -1, slots.shape[-1])
    return lax.all_to_all(split_up, AXES, 0, 0, tiled=True).reshape(slots.shape)


def body(right_sides, tiles, tile_cols, send_rows, block_inverse, coarse_basis, coarse_inverse):
    blocks, rhs, order = right_sides.shape
    rows, total = coarse_inverse.shape
    halo = send_rows.shape[1]
    count = lax.axis_size("sx") * lax.axis_size("sy")
    field = (right_sides.shape, F32)
    sends = pltpu.SMEM((halo, send_rows.shape[0]), jnp.int32)
    turned_sends = send_rows.T
    extended = pltpu.VMEM((blocks + 4 * halo, rhs, order), BF)

    def sems(number):
        return pltpu.SemaphoreType.DMA((number,))

    def swapped(values):
        return [swap(value, number, odd) for value, (number, odd) in zip(values, SWAPS)]

    slots, right, inverses, basis, coarse_rows, *halos = call(
        start_kernel,
        (turned_sends, right_sides, block_inverse, coarse_basis, coarse_inverse),
        "hhhhh>hvvvvhhhh",
        [
            ((count * SLOT, LANES), BF),
            field,
            (block_inverse.shape, BF),
            (coarse_basis.shape, BF),
            (coarse_inverse.shape, BF),
        ]
        + [((rhs, total + 2 * halo * order), BF)] * 4,
        (
            pltpu.VMEM((count * SLOT, LANES), BF),
            pltpu.VMEM((4, rhs, total + 2 * halo * order), BF),
            sends,
            pltpu.VMEM(coarse_inverse.shape, F32),
            sems(5),
            sems(5),
        ),
    )
    halos = swapped(halos)
    early, late = halos[: EARLY[0]], halos[EARLY[0] :]
    arrived = exchange(slots)
    reach = blocks + halo * EARLY[0]
    coarse_rows, bases, locals_, blocks_of_a, tile_cols, turned_sends, local = call(
        gather_kernel,
        (coarse_rows, basis, right, inverses, tiles, tile_cols, turned_sends, *early),
        "vvvvhhh" + "v" * len(early) + ">vvvvvvv",
        [
            (((1 + EARLY[0]) * rows, total), BF),
            ((reach,) + coarse_basis.shape[1:], BF),
            ((max(reach - blocks, 1), rhs, order), BF),
            (tiles.shape, BF),
            (tile_cols.shape, jnp.int32),
            (turned_sends.shape, jnp.int32),
            field,
        ],
        (sems(2), sems(blocks)),
        flops=10**11 if EARLY[0] else None,
    )
    slots, update, image, *nexts = call(
        first_kernel,
        (tile_cols, turned_sends, arrived, coarse_rows, bases, local, locals_, inverses, right, blocks_of_a, *late),
        "vvvvvvvvvv" + "v" * len(late) + ">hvvhhhh",
        [((count * 2 * SLOT, LANES), BF), ((blocks + 4 * halo, rhs, order), F32), field]
        + [((rhs, halo * order), BF)] * 4,
        (
            pltpu.VMEM((count * 2 * SLOT, LANES), BF),
            pltpu.VMEM((4, rhs, halo * order), BF),
            extended,
            sems(5),
        ),
    )
    nexts = swapped(nexts)
    soon, nexts = nexts[: EARLY[1]], nexts[EARLY[1] :]
    arrived = exchange(slots)
    (local,) = call(
        local_kernel,
        (image, inverses, *soon),
        "vv" + "v" * len(soon) + ">v",
        [((blocks + halo * EARLY[1], rhs, order), F32)],
        flops=10**11 if EARLY[1] else None,
    )
    slots, scaled, second, residual, image = call(
        second_kernel,
        (tile_cols, arrived, coarse_rows, bases, local, update, image, right, blocks_of_a, *late, *nexts),
        "vvvvvvvvv" + "v" * (len(late) + len(nexts)) + ">vvvvv",
        [((count, 1, LANES), F32)] + [field] * 4,
        (extended,),
    )
    return tuple(call(last_kernel, (exchange(slots), scaled, second, residual, image), "vvvvv>vv", [field] * 2))


def solution(mesh):
    block3 = P(AXES, None, None)
    placed = (block3, P(AXES, None, None, None), P(AXES, None), P(AXES, None), block3, block3, P(AXES, None))
    return jax.shard_map(body, mesh=mesh, in_specs=placed, out_specs=(block3, block3), check_vma=False)
```

```python
import functools

import jax
import jax.numpy as jnp
from jax import lax
from jax.experimental import pallas as pl
from jax.experimental.pallas import tpu as pltpu
from jax.sharding import PartitionSpec as P

AXES = ("sx", "sy")
BF = jnp.bfloat16
F32 = jnp.float32
NT = (((1,), (1,)), ((), ()))
LANES = 128
SLOT = 8
SWAPS = ((1, True), (0, True), (1, False), (0, False))
EARLY = 1, 0


def swap(value, number, odd):
    counts = [lax.axis_size(axis) for axis in AXES]
    pairs = []
    for device in range(counts[0] * counts[1]):
        place = list(divmod(device, counts[1]))
        other = place[number] + (1 if (place[number] % 2 == 0) != odd else -1)
        if 0 <= other < counts[number]:
            place[number] = other
        else:
            place[1 - number] ^= 2 if number == 0 and counts[1] % 4 == 0 else 1
        pairs.append((device, place[0] * counts[1] + place[1]))
    return lax.ppermute(value, AXES, pairs)


def swap_ends(number, odd):
    axis = AXES[number]
    place, count = lax.axis_index(axis), lax.axis_size(axis)
    up = (lax.rem(place, 2) == 0) != odd
    send = 2 * number + jnp.where(up, 0, 1)
    slot = 2 * number + jnp.where(up, 1, 0)
    valid = jnp.where(up, place < count - 1, place > 0)
    return send, slot, valid


def split(value):
    high = value.astype(BF)
    return high, (value - high.astype(F32)).astype(BF)


def restrict_slot(vectors, basis_ref, parts=2):
    left, right = [], []
    for b, vector in enumerate(vectors):
        for part in split(vector)[:parts]:
            left.append(basis_ref[b])
            right.append(jnp.concatenate([part] * 4, axis=0))
    full = lax.dot_general(
        jnp.concatenate(left, axis=1), jnp.concatenate(right, axis=1), NT, preferred_element_type=F32
    )
    group = lax.broadcasted_iota(jnp.int32, (SLOT, LANES), 1) // 32
    slot = full[:SLOT]
    for j in range(1, 4):
        slot = jnp.where(group == j, full[SLOT * j : SLOT * (j + 1)], slot)
    return slot


def coarse_parts(arrived, inverses):
    count = arrived.shape[0]
    lane = lax.broadcasted_iota(jnp.int32, (1, 4, SLOT, LANES), 3) // 32
    part = lax.broadcasted_iota(jnp.int32, (1, 4, SLOT, LANES), 1)
    spread_out = jnp.where(lane == part, arrived[:, None], 0.0)
    column = spread_out.reshape(count * 4 * SLOT, LANES).astype(BF)
    product = jnp.dot(inverses, column, preferred_element_type=F32)
    parts = []
    for s in range(inverses.shape[0] // 32):
        turned = product[32 * s : 32 * (s + 1)].T
        parts.append((turned[:32] + turned[32:64] + turned[64:96] + turned[96:]).astype(BF))
    return parts


def local_product(vector, inverse):
    rows = vector.shape[0]
    both = lax.dot_general(jnp.concatenate(split(vector), axis=0), inverse, NT, preferred_element_type=F32)
    return both[:rows] + both[rows:]


def image_blocks(extended, tiles, cols):
    blocks, width = tiles.shape[:2]
    rhs, order = extended.shape[1:]
    images = []
    for b in range(0, blocks, 2):
        pair = range(b, min(b + 2, blocks))
        vectors = [
            jnp.concatenate([extended[x]] + [extended[cols[x, t]] for t in range(width - 1)], axis=1) for x in pair
        ]
        rows = [jnp.concatenate([tiles[x, t] for t in range(width)], axis=1) for x in pair]
        both = lax.dot_general(
            jnp.concatenate(vectors, axis=0), jnp.concatenate(rows, axis=0), NT, preferred_element_type=F32
        )
        for k in range(len(pair)):
            images.append(both[rhs * k : rhs * (k + 1), order * k : order * (k + 1)])
    return images


def sums_row(upper, lower):
    return jnp.sum(jnp.concatenate([upper, lower, upper, lower], axis=0).T, axis=0, keepdims=True)


def repeated(slot, shape):
    return jnp.broadcast_to(slot[None], (shape[0] // slot.shape[0],) + slot.shape).reshape(shape).astype(BF)


def chosen(sends, m, direction):
    return sum(jnp.where(direction == k, sends[m, k], 0) for k in range(sends.shape[1]))


def fetch(pairs, sems):
    copies = [pltpu.make_async_copy(source, target, sems.at[k]) for k, (source, target) in enumerate(pairs)]
    for copy in copies:
        copy.start()
    return copies


def start_kernel(
    send_hbm, right_hbm, block_inverse_hbm, basis_hbm, inverse_hbm,
    slot_hbm, right_ref, block_inverse_ref, basis_ref, inverse_ref, out0, out1, out2, out3,
    slot_ref, out_ref, send_ref, wide, sems, out_sems,
):
    copies = fetch(
        [
            (right_hbm, right_ref),
            (basis_hbm, basis_ref),
            (block_inverse_hbm, block_inverse_ref),
            (inverse_hbm, wide),
            (send_hbm, send_ref),
        ],
        sems,
    )
    blocks, rhs, order = right_ref.shape
    halo = send_ref.shape[0]
    total = wide.shape[1]
    for copy in copies[:2]:
        copy.wait()
    vectors = [right_ref[b] for b in range(blocks)]
    slot_ref[...] = repeated(restrict_slot(vectors, basis_ref, 1), slot_ref.shape)
    leaving = fetch([(slot_ref, slot_hbm)], out_sems)
    copies[3].wait()
    inverse = wide[...].astype(BF)
    inverse_ref[...] = inverse
    copies[2].wait()
    copies[4].wait()
    for q, ((number, odd), out_hbm) in enumerate(zip(SWAPS, (out0, out1, out2, out3))):
        send, _, _ = swap_ends(number, odd)
        out_ref[q, :, :total] = inverse
        for m in range(halo):
            row = send_ref[m, send]
            out_ref[q, :, total + m * order : total + (m + 1) * order] = basis_ref[row]
            start = total + (halo + m) * order
            local = local_product(right_ref[row], block_inverse_ref[row])
            out_ref[q, :, start : start + order] = local.astype(BF)
        leaving += fetch([(out_ref.at[q], out_hbm)], out_sems.at[pl.ds(1 + q, 1)])
    for copy in leaving:
        copy.wait()


def gather_kernel(inverse_ref, basis_ref, right_ref, block_inverse_ref, tiles_hbm, cols_hbm, send_hbm, *refs):
    halos, refs = refs[: EARLY[0]], refs[EARLY[0] :]
    inverses_ref, bases_ref, locals_ref, tiles_ref, cols_ref, send_ref, local_ref, sems, tile_sems = refs
    rows, total = inverse_ref.shape
    blocks, _, order = basis_ref.shape
    copies = fetch([(cols_hbm, cols_ref), (send_hbm, send_ref)], sems)
    copies += fetch([(tiles_hbm.at[b], tiles_ref.at[b]) for b in range(tiles_ref.shape[0])], tile_sems)
    for b in range(blocks):
        local_ref[b] = local_product(right_ref[b], block_inverse_ref[b])
    inverses_ref[:rows] = inverse_ref[...]
    bases_ref[:blocks] = basis_ref[...]
    for q, ref in enumerate(halos):
        inverses_ref[rows * (1 + q) : rows * (2 + q)] = ref[:, :total]
        halo = (ref.shape[1] - total) // (2 * order)
        for m in range(halo):
            at = total + m * order
            bases_ref[blocks + halo * q + m] = ref[:, at : at + order]
            at += halo * order
            locals_ref[halo * q + m] = ref[:, at : at + order]
    for copy in copies:
        copy.wait()


def all_inverses(inverses_ref, late):
    total = inverses_ref.shape[1]
    return jnp.concatenate([inverses_ref[...]] + [ref[:, :total] for ref in late], axis=0)


def basis_block(k, bases_ref, late, total, halo):
    if k < bases_ref.shape[0]:
        return bases_ref[k]
    q, m = divmod(k - bases_ref.shape[0], halo)
    order = bases_ref.shape[2]
    return late[q][:, total + m * order : total + (m + 1) * order]


def pack(extended, k, value, blocks, halo):
    if k < blocks:
        extended[k] = value.astype(BF)
    else:
        q, m = divmod(k - blocks, halo)
        _, slot, valid = swap_ends(*SWAPS[q])
        extended[blocks + halo * slot + m] = jnp.where(valid, value, 0.0).astype(BF)


def spreads(coarse, bases, blocks, halo):
    out, k = [], 0
    while k < len(bases):
        s = owner(k, blocks, halo)
        pair = 2 if k + 1 < len(bases) and owner(k + 1, blocks, halo) == s else 1
        order = bases[k].shape[1]
        both = jnp.dot(coarse[s], jnp.concatenate(bases[k : k + pair], axis=1), preferred_element_type=F32)
        out += [both[:, order * m : order * (m + 1)] for m in range(pair)]
        k += pair
    return out


def owner(k, blocks, halo):
    return 0 if k < blocks else 1 + (k - blocks) // halo


def first_kernel(
    cols_ref, send_ref, arrived_ref, inverses_ref, bases_ref, local_ref, locals_ref, block_inverse_ref, right_ref,
    tiles_ref, *refs,
):
    late, refs = refs[: 4 - EARLY[0]], refs[4 - EARLY[0] :]
    slot_hbm, update_ref, image_ref, out0, out1, out2, out3 = refs[:7]
    slot_ref, out_ref, extended, out_sems = refs[7:]
    cols, sends = cols_ref[...], send_ref[...]
    blocks, rhs, order = right_ref.shape
    halo = sends.shape[0]
    total = inverses_ref.shape[1]
    arrived = arrived_ref[...].astype(F32).reshape(-1, SLOT, LANES)
    coarse = coarse_parts(arrived, all_inverses(inverses_ref, late))
    early = blocks + halo * EARLY[0]
    bases = [basis_block(k, bases_ref, late, total, halo) for k in range(update_ref.shape[0])]
    spread = spreads(coarse, bases, blocks, halo)
    for k in range(update_ref.shape[0]):
        if k < blocks:
            local = local_ref[k]
        elif k < early:
            local = locals_ref[k - blocks].astype(F32)
        else:
            q, m = divmod(k - early, halo)
            at = total + (halo + m) * order
            local = late[q][:, at : at + order].astype(F32)
        update = local + spread[k]
        update_ref[k] = update
        pack(extended, k, update, blocks, halo)
    upper = lower = jnp.zeros((rhs, order), F32)
    images = image_blocks(extended, tiles_ref, cols)
    for b, image in enumerate(images):
        image_ref[b] = image
        upper += right_ref[b] * image
        lower += image * image
    row = sums_row(upper, lower)
    high, low = split(row)
    lane = lax.broadcasted_iota(jnp.int32, (1, LANES), 1)
    row = jnp.where(lane < 64, high.astype(F32), low.astype(F32))
    whole = jnp.concatenate([restrict_slot(images, bases_ref), jnp.broadcast_to(row, (SLOT, LANES))], axis=0)
    slot_ref[...] = repeated(whole, slot_ref.shape)
    leaving = fetch([(slot_ref, slot_hbm)], out_sems)
    for q, ((number, odd), out_hbm) in enumerate(zip(SWAPS, (out0, out1, out2, out3))):
        send, _, _ = swap_ends(number, odd)
        for m in range(halo):
            row = chosen(sends, m, send)
            local = local_product(image_ref[row], block_inverse_ref[row])
            out_ref[q, :, m * order : (m + 1) * order] = local.astype(BF)
        leaving += fetch([(out_ref.at[q], out_hbm)], out_sems.at[pl.ds(1 + q, 1)])
    for copy in leaving:
        copy.wait()


def local_kernel(image_ref, block_inverse_ref, *refs):
    blocks, _, order = image_ref.shape
    local_ref = refs[-1]
    for b in range(blocks):
        local_ref[b] = local_product(image_ref[b], block_inverse_ref[b])
    for q, ref in enumerate(refs[:-1]):
        halo = ref.shape[1] // order
        for m in range(halo):
            local_ref[blocks + halo * q + m] = ref[:, m * order : (m + 1) * order].astype(F32)


def second_kernel(
    cols_ref, arrived_ref, inverses_ref, bases_ref, local_ref, update_ref, image_ref, right_ref, tiles_ref, *refs,
):
    late, refs = refs[: 4 - EARLY[0]], refs[4 - EARLY[0] :]
    nexts, refs = refs[: 4 - EARLY[1]], refs[4 - EARLY[1] :]
    slot_ref, scaled_ref, second_ref, residual_ref, image2_ref, extended = refs
    cols = cols_ref[...]
    blocks, rhs, order = right_ref.shape
    halo = (update_ref.shape[0] - blocks) // 4
    total = inverses_ref.shape[1]
    arrived = arrived_ref[...].astype(F32).reshape(-1, 2 * SLOT, LANES)
    coarse = coarse_parts(arrived[:, :SLOT], all_inverses(inverses_ref, late))
    sums = jnp.sum(arrived[:, SLOT : SLOT + 1], axis=0)
    turned = jnp.broadcast_to(sums, (LANES, LANES)).T
    weight = (turned[:32] + turned[64:96]) / (turned[32:64] + turned[96:] + 1e-6)
    bases = [basis_block(k, bases_ref, late, total, halo) for k in range(update_ref.shape[0])]
    spread = spreads(coarse, bases, blocks, halo)
    for k in range(update_ref.shape[0]):
        if k < local_ref.shape[0]:
            local = local_ref[k]
        else:
            q, m = divmod(k - local_ref.shape[0], halo)
            local = nexts[q][:, m * order : (m + 1) * order].astype(F32)
        update = update_ref[k]
        second = update - weight * (local + spread[k])
        if k < blocks:
            scaled_ref[k] = weight * update
            second_ref[k] = second
        pack(extended, k, second, blocks, halo)
    upper = lower = jnp.zeros((rhs, order), F32)
    for b, image in enumerate(image_blocks(extended, tiles_ref, cols)):
        residual = right_ref[b] - weight * image_ref[b]
        residual_ref[b] = residual
        image2_ref[b] = image
        upper += residual * image
        lower += image * image
    slot_ref[...] = jnp.broadcast_to(sums_row(upper, lower)[None], slot_ref.shape)


def last_kernel(arrived_ref, scaled_ref, second_ref, residual_ref, image_ref, solution_ref, out_ref):
    sums = jnp.sum(arrived_ref[...], axis=0)
    turned = jnp.broadcast_to(sums, (LANES, LANES)).T
    weight = turned[:32] / (turned[32:64] + 1e-6)
    for b in range(scaled_ref.shape[0]):
        solution_ref[b] = scaled_ref[b] + weight * second_ref[b]
        out_ref[b] = residual_ref[b] - weight * image_ref[b]


def call(kernel, inputs, places, outputs, scratch=(), flops=None):
    kinds = {"v": pltpu.VMEM, "h": pltpu.HBM}
    into, out = places.split(">")
    inputs = [pltpu.with_memory_space_constraint(x, pltpu.HBM) if p == "h" else x for x, p in zip(inputs, into)]
    return pl.pallas_call(
        kernel,
        out_shape=[
            pltpu.HBM(shape, dtype) if p == "h" else jax.ShapeDtypeStruct(shape, dtype)
            for (shape, dtype), p in zip(outputs, out)
        ],
        in_specs=[pl.BlockSpec(memory_space=kinds[p]) for p in into],
        out_specs=[pl.BlockSpec(memory_space=kinds[p]) for p in out],
        scratch_shapes=scratch,
        compiler_params=pltpu.CompilerParams(vmem_limit_bytes=32 * 1024 * 1024),
        cost_estimate=flops and pl.CostEstimate(flops=flops, bytes_accessed=0, transcendentals=0),
        name=kernel.__name__,
    )(*inputs)


def exchange(slots):
    count = lax.axis_size("sx") * lax.axis_size("sy")
    split_up = slots.reshape(count, -1, slots.shape[-1])
    return lax.all_to_all(split_up, AXES, 0, 0, tiled=True).reshape(slots.shape)


def body(right_sides, tiles, tile_cols, send_rows, block_inverse, coarse_basis, coarse_inverse):
    blocks, rhs, order = right_sides.shape
    rows, total = coarse_inverse.shape
    halo = send_rows.shape[1]
    count = lax.axis_size("sx") * lax.axis_size("sy")
    field = (right_sides.shape, F32)
    sends = pltpu.SMEM((halo, send_rows.shape[0]), jnp.int32)
    turned_sends = send_rows.T
    extended = pltpu.VMEM((blocks + 4 * halo, rhs, order), BF)

    def sems(number):
        return pltpu.SemaphoreType.DMA((number,))

    def swapped(values):
        return [swap(value, number, odd) for value, (number, odd) in zip(values, SWAPS)]

    slots, right, inverses, basis, coarse_rows, *halos = call(
        start_kernel,
        (turned_sends, right_sides, block_inverse, coarse_basis, coarse_inverse),
        "hhhhh>hvvvvhhhh",
        [
            ((count * SLOT, LANES), BF),
            field,
            (block_inverse.shape, BF),
            (coarse_basis.shape, BF),
            (coarse_inverse.shape, BF),
        ]
        + [((rhs, total + 2 * halo * order), BF)] * 4,
        (
            pltpu.VMEM((count * SLOT, LANES), BF),
            pltpu.VMEM((4, rhs, total + 2 * halo * order), BF),
            sends,
            pltpu.VMEM(coarse_inverse.shape, F32),
            sems(5),
            sems(5),
        ),
    )
    halos = swapped(halos)
    early, late = halos[: EARLY[0]], halos[EARLY[0] :]
    arrived = exchange(slots)
    reach = blocks + halo * EARLY[0]
    coarse_rows, bases, locals_, blocks_of_a, tile_cols, turned_sends, local = call(
        gather_kernel,
        (coarse_rows, basis, right, inverses, tiles, tile_cols, turned_sends, *early),
        "vvvvhhh" + "v" * len(early) + ">vvvvvvv",
        [
            (((1 + EARLY[0]) * rows, total), BF),
            ((reach,) + coarse_basis.shape[1:], BF),
            ((max(reach - blocks, 1), rhs, order), BF),
            (tiles.shape, BF),
            (tile_cols.shape, jnp.int32),
            (turned_sends.shape, jnp.int32),
            field,
        ],
        (sems(2), sems(blocks)),
        flops=10**11 if EARLY[0] else None,
    )
    slots, update, image, *nexts = call(
        first_kernel,
        (tile_cols, turned_sends, arrived, coarse_rows, bases, local, locals_, inverses, right, blocks_of_a, *late),
        "vvvvvvvvvv" + "v" * len(late) + ">hvvhhhh",
        [((count * 2 * SLOT, LANES), BF), ((blocks + 4 * halo, rhs, order), F32), field]
        + [((rhs, halo * order), BF)] * 4,
        (
            pltpu.VMEM((count * 2 * SLOT, LANES), BF),
            pltpu.VMEM((4, rhs, halo * order), BF),
            extended,
            sems(5),
        ),
    )
    nexts = swapped(nexts)
    soon, nexts = nexts[: EARLY[1]], nexts[EARLY[1] :]
    arrived = exchange(slots)
    (local,) = call(
        local_kernel,
        (image, inverses, *soon),
        "vv" + "v" * len(soon) + ">v",
        [((blocks + halo * EARLY[1], rhs, order), F32)],
        flops=10**11 if EARLY[1] else None,
    )
    slots, scaled, second, residual, image = call(
        second_kernel,
        (tile_cols, arrived, coarse_rows, bases, local, update, image, right, blocks_of_a, *late, *nexts),
        "vvvvvvvvv" + "v" * (len(late) + len(nexts)) + ">vvvvv",
        [((count, 1, LANES), F32)] + [field] * 4,
        (extended,),
    )
    return tuple(call(last_kernel, (exchange(slots), scaled, second, residual, image), "vvvvv>vv", [field] * 2))


def solution(mesh):
    block3 = P(AXES, None, None)
    placed = (block3, P(AXES, None, None, None), P(AXES, None), P(AXES, None), block3, block3, P(AXES, None))
    return jax.shard_map(body, mesh=mesh, in_specs=placed, out_specs=(block3, block3), check_vma=False)
```
